32 devices in a mesh: gx: 4 (over z), gy: 8 (over y, x, core).
Axes of the slice: x: 2, y: 2, z: 4, core: 2. Of those that a mesh axis runs over, the one named last changes fastest.
Arguments:
- coords: float32 [1, 3, 8, 16, 128], P(None, None, 'gx', 'gy'), may hold values from 0 to 1
- kinds: int32 [8, 16, 128], P('gx', 'gy'), may hold values from 0 to 2
- forces: bfloat16 [1, 3, 8, 16, 128], P(None, None, 'gx', 'gy'), may hold values from -4 to 4
- tile_offsets: int32 [1, 8, 16, 8], P(None, 'gx', 'gy'), may hold values from 0 to 8, as said below
- tile_mask: int32 [1, 8, 16, 8], P(None, 'gx', 'gy'), may hold values 0 or 1
Outputs:
- gram: float32 [1, 1536, 1536], P(None, 'gy')
- rhs: float32 [1, 1536], P(None, 'gy')
The draws below stay inside these ranges and needn't reach their ends.
Inputs may be any that keep to these rules, and one draw needn't show every extreme that they name: `tile_offsets`: for one frame and block the 8 entries are distinct; entry o names the block o // 3 - 1 steps along the first direction and o % 3 - 1 along the second, periodically.
All inputs are finite; a program needn't handle non-finite values. No bound on the sum of `tile_mask` on one device may be relied on, other than what follows from the above.
Results may differ from the reference program's by a relative error of at most 0.0013.
Values sent between devices are 32-bit elements; how exact they have to be, the bound alone decides.
No kernel may reach another device: no remote copies, remote signals or barrier semaphores. Data moves between devices by JAX's collectives and lax.ppermute only.
A program may use at most 128 MiB of HBM per device.

```python
import math
import jax
import jax.numpy as jnp
from jax import lax

K = 256
PAIRS = 6
BEADS = 128
FRAMES = 1
NT = 8
NBX = 8
NBY = 16


def bead_pairs(key, phase_lo, phase_hi, strength):
    half = BEADS // 2
    shape = (FRAMES, 1, NBX, NBY, half)
    keys = jax.random.split(key, 8)
    base = jax.random.uniform(keys[0], (FRAMES, 3, NBX, NBY, half), jnp.float32)
    cosine = jax.random.uniform(keys[1], shape, jnp.float32, -1.0, 1.0)
    turn = jax.random.uniform(keys[2], shape, jnp.float32, -math.pi, math.pi)
    sine = jnp.sqrt(jnp.maximum(1.0 - cosine * cosine, 0.0))
    unit = jnp.concatenate([sine * jnp.cos(turn), sine * jnp.sin(turn), cosine], axis=1)
    twin = jax.random.randint(keys[3], shape, 0, 10, dtype=jnp.int32) < 3
    close = jax.random.uniform(keys[4], shape, jnp.float32, 0.003, 0.026)
    bins = jax.random.randint(keys[5], shape, K // 16, K * 27 // 64, dtype=jnp.int32).astype(jnp.float32)
    phase = jax.random.uniform(keys[6], shape, jnp.float32, phase_lo, phase_hi)
    bonded = (bins + 0.5 + phase) / K
    length = jnp.where(twin, close, bonded)
    step = length * unit
    forward = base + step
    partner = jnp.where((forward >= 0.0) & (forward <= 1.0), forward, base - step)
    along = (base - partner) / length
    positions = jnp.stack([base, partner], axis=-1).reshape(FRAMES, 3, NBX, NBY, BEADS)
    pushes = jnp.stack([strength * along, -strength * along], axis=-1).reshape(FRAMES, 3, NBX, NBY, BEADS)
    scores = jax.random.randint(keys[7], (FRAMES, 1, NBX, NBY, BEADS), 0, 1048576, dtype=jnp.int32)
    scores = scores * BEADS + jnp.arange(BEADS, dtype=jnp.int32)
    order = jnp.broadcast_to(jnp.argsort(scores, axis=-1), positions.shape)
    positions = jnp.take_along_axis(positions, order, axis=-1)
    pushes = jnp.take_along_axis(pushes, order, axis=-1)
    return (positions, pushes)


def draw_coords(key, part):
    positions, pushes = bead_pairs(key, 0.05, 0.35, 1.5)
    return positions.astype(jnp.float32)


def draw_forces(key, part):
    shape = (FRAMES, 3, NBX, NBY, BEADS)
    positions, pushes = bead_pairs(key, 0.05, 0.35, 1.5)
    key = jax.random.fold_in(key, 7)
    noise = 0.6 * jnp.clip(jax.random.normal(key, shape, jnp.float32), -4.0, 4.0)
    return (pushes + noise).astype(jnp.bfloat16)


def draw_tile_offsets(key, part):
    key = jax.random.fold_in(key, 5)
    scores = jax.random.randint(key, (FRAMES, NBX, NBY, 9), 0, 1048576, dtype=jnp.int32)
    scores = scores * 16 + jnp.arange(9, dtype=jnp.int32)
    order = jnp.argsort(scores, axis=-1)
    return order[..., :NT].astype(jnp.int32)


def place_ends(array, stream_key, least, largest):
    extent = array.shape
    place = [jax.random.randint(jax.random.fold_in(stream_key, axis), (), 0, extent[axis]) for axis in range(len(extent))]
    array = array.at[tuple(place)].set(least)
    longest = extent.index(max(extent))
    place[longest] = (place[longest] + 1) % extent[longest]
    return array.at[tuple(place)].set(largest)


def setup_inputs(seed: int = 0) -> dict:
    key_of = jax.random.split(jax.random.key(seed), 6)
    coords = draw_coords(jax.random.fold_in(key_of[5], 71), 0)
    kinds = place_ends(jax.random.randint(key_of[1], (NBX, NBY, BEADS), 0, 3), jax.random.fold_in(key_of[1], 1), 0, 2).astype(jnp.int32)
    forces = draw_forces(jax.random.fold_in(key_of[5], 71), 0)
    tile_offsets = draw_tile_offsets(jax.random.fold_in(key_of[5], 71), 0)
    tile_mask = place_ends((jax.random.randint(key_of[4], (FRAMES, NBX, NBY, NT), 0, 4) < 3).astype(jnp.int32), jax.random.fold_in(key_of[4], 1), 0, 1)
    return {"coords": coords, "kinds": kinds, "forces": forces, "tile_offsets": tile_offsets, "tile_mask": tile_mask}


RCUT = 1.0
SOFT = 0.05

def radial(r2):
    dist = jnp.sqrt(r2)
    centers = RCUT * (jnp.arange(K, dtype=jnp.float32) + 0.5) / K
    spread = RCUT / K
    taper = jnp.square(jnp.maximum(1.0 - r2 / (RCUT * RCUT), 0.0))
    scaled = (dist[..., None] - centers) / spread
    return (jnp.exp(-0.5 * scaled * scaled) * taper[..., None]).astype(jnp.bfloat16)

def couplings(center, source, kind_center, kind_source, offset, live):
    beads = center.shape[1]
    shift = jnp.stack([offset // 3 - 1, offset % 3 - 1, 0 * offset]).astype(jnp.float32)
    delta = center[:, :, None] - source[:, None, :] - shift[:, None, None]
    r2 = lax.optimization_barrier(jnp.sum(delta * delta, axis=0))
    lower_kind = jnp.minimum(kind_center[:, None], kind_source[None, :])
    upper_kind = jnp.maximum(kind_center[:, None], kind_source[None, :])
    pair_kind = lower_kind * (5 - lower_kind) // 2 + upper_kind
    select = (pair_kind[None] == jnp.arange(PAIRS, dtype=jnp.int32)[:, None, None]).astype(jnp.float32)
    scale = live.astype(jnp.float32) / jnp.sqrt(r2 + SOFT)
    weight = (delta[:, None] * select[None] * scale[None, None]).reshape(3 * PAIRS, beads, beads)
    return (weight.astype(jnp.bfloat16), radial(r2))

def reference(coords, kinds, forces, tile_offsets, tile_mask):
    beads = BEADS
    frame_rows = 3 * BEADS * NBX * NBY

    def target(carry, index):
        gram, rhs = carry
        frame = index // (NBX * NBY)
        rest = index % (NBX * NBY)
        xpos = rest // NBY
        ypos = rest % NBY
        center = coords[frame, :, xpos, ypos, :]
        kind_center = kinds[xpos, ypos, :]
        design = jnp.zeros((beads, 3 * PAIRS, K), jnp.float32)
        for slot in range(NT):
            offset = tile_offsets[frame, xpos, ypos, slot]
            src_x = (xpos + offset // 3 - 1) % NBX
            src_y = (ypos + offset % 3 - 1) % NBY
            source = coords[frame, :, src_x, src_y, :]
            kind_source = kinds[src_x, src_y, :]
            weight, basis = couplings(center, source, kind_center, kind_source, offset, tile_mask[frame, xpos, ypos, slot])
            design = design + jnp.einsum('cij,ijk->ick', weight.astype(jnp.float32), basis.astype(jnp.float32))
        rows = design.astype(jnp.bfloat16).reshape(beads * 3, PAIRS * K)
        target_force = forces[frame, :, xpos, ypos, :].T.reshape(beads * 3)
        gram = gram.at[frame].add(jnp.dot(rows.T, rows, preferred_element_type=jnp.float32))
        rhs = rhs.at[frame].add(jnp.dot(target_force, rows, preferred_element_type=jnp.float32))
        return ((gram, rhs), None)
    start = (jnp.zeros((FRAMES, PAIRS * K, PAIRS * K), jnp.float32), jnp.zeros((FRAMES, PAIRS * K), jnp.float32))
    (gram, rhs), _ = lax.scan(target, start, jnp.arange(FRAMES * NBX * NBY, dtype=jnp.int32))
    return (gram / frame_rows, rhs / frame_rows)
```

```python
import functools
import math
import jax
import jax.numpy as jnp
from jax import lax
from jax.experimental import pallas as pl
from jax.experimental.pallas import tpu as pltpu
from jax.sharding import PartitionSpec as P

K=256; PAIRS=6
STEP=32; SPAN=64
ROOT=math.sqrt(0.5*math.log2(math.e))
NEG=-1e9

def design_kernel(off_ref, mask_ref, rows_ref, kind_ref, col_ref, out_ref, pos_s, lt_s, code_s, w_s, res_s, list_s, *, by_blocks, beads, slots, unroll):
    b = pl.program_id(0)
    bx = b // by_blocks
    by = b % by_blocks
    live = jnp.int32(0)
    for t in range(slots):
        list_s[live] = off_ref[b, t]
        live = live + mask_ref[b, t]
    chunks = (live + 1) // 2
    colv = [jnp.broadcast_to(col_ref[0, :, a:a+1], (beads, beads)) for a in range(3)]
    def geom(s, c):
        o = list_s[s]
        ox = o // 3
        oy = o % 3
        src = (bx + ox) * (by_blocks + 2) + by + oy
        sx = (ox - 1).astype(jnp.float32)
        sy = (oy - 1).astype(jnp.float32)
        d0 = colv[0] - rows_ref[src, 0:1, :] - sx
        d1 = colv[1] - rows_ref[src, 1:2, :] - sy
        d2 = colv[2] - rows_ref[src, 2:3, :]
        r2 = d0 * d0 + d1 * d1 + d2 * d2
        u = jnp.sqrt(r2) * K
        m = jnp.minimum(jnp.floor(u * (1.0 / STEP)), K // STEP - 1.0)
        pos_s[s] = (u - m * STEP) * ROOT
        t = jnp.maximum(1.0 - r2, 0.0)
        lt_s[s] = jnp.where(t > 0.0, 2.0 * jnp.log2(jnp.where(t > 0.0, t, 1.0)), NEG)
        code_s[s] = kind_ref[src, 0:1, :] * 8.0 + m
        sc = 1.0 / jnp.sqrt(r2 + 0.05)
        w_s[0, s] = d0 * sc
        w_s[1, s] = d1 * sc
        w_s[2, s] = d2 * sc
        return c
    lax.fori_loop(0, live, geom, 0)
    @pl.when(live % 2 == 1)
    def _():
        z = jnp.zeros((beads, beads), jnp.float32)
        pos_s[live] = z
        lt_s[live] = z + NEG
        code_s[live] = z
        for a in range(3):
            w_s[a, live] = z

    cen = (lax.broadcasted_iota(jnp.int32, (SPAN, beads), 0).astype(jnp.float32) - 15.5) * ROOT
    row24 = lax.broadcasted_iota(jnp.int32, (24, beads), 0).astype(jnp.float32)

    def one(i, n):
        gs = []
        ws = []
        for s in range(n):
            x = pos_s[s, pl.ds(i, 1), :] - cen
            g = jnp.exp2(lt_s[s, pl.ds(i, 1), :] - x * x).astype(jnp.bfloat16)
            gs.append(g)
            hit = code_s[s, pl.ds(i, 1), :] == row24
            w = [jnp.where(hit, w_s[a, s, pl.ds(i, 1), :], 0.0) for a in range(3)]
            ws.append(jnp.concatenate(w, axis=0).astype(jnp.bfloat16))
        g = jnp.concatenate(gs, axis=1)
        w = jnp.concatenate(ws, axis=1)
        r = lax.dot_general(w, g, (((1,), (1,)), ((), ())), preferred_element_type=jnp.float32)
        res_s[pl.ds(pl.multiple_of(i * 72, 8), 72), 0:SPAN] = r

    for c in range(1, slots // 2 + 1):
        @pl.when(chunks == c)
        def _(c=c):
            def body(i, carry):
                for q in range(unroll):
                    one(i * unroll + q, 2 * c)
                return carry
            lax.fori_loop(0, beads // unroll, body, 0)
    @pl.when(chunks == 0)
    def _():
        res_s[...] = jnp.zeros_like(res_s)

    lane = lax.broadcasted_iota(jnp.int32, (8, 128), 1)
    low64 = lane < 64
    def unfold(g, carry):
        i0 = g * 16
        kt16 = jnp.broadcast_to(col_ref[0, pl.ds(pl.multiple_of(i0, 16), 16), 3:4], (16, 128))
        for a in range(3):
            d = []
            for t in range(3):
                halves = []
                for h in range(2):
                    rr = [res_s[pl.ds((i0 + h * 8) * 72 + a * 24 + t * 8 + m, 8, stride=72), :] for m in range(8)]
                    pair = lambda p, q: jnp.where(low64, p, pltpu.roll(q, 64, 1))
                    e0, e1 = pair(rr[0], rr[2]), pair(rr[4], rr[6])
                    o0, o1 = pair(rr[1], rr[3]), pair(rr[5], rr[7])
                    e0, e1 = pltpu.roll(e0, 112, 1), pltpu.roll(e1, 112, 1)
                    o0, o1 = pltpu.roll(o0, 16, 1), pltpu.roll(o1, 16, 1)
                    lo = jnp.where(lane < 112, e0, e1) + jnp.where(lane < 16, 0.0, o0)
                    hi = jnp.where(lane < 112, e1, 0.0) + jnp.where(lane < 16, o0, o1)
                    halves.append((lo, hi))
                d.append([jnp.concatenate([halves[0][v], halves[1][v]], axis=0) for v in range(2)])
            is_t = [kt16 == float(t) for t in range(3)]
            for p, (lo_t, hi_t) in enumerate([(0, 0), (0, 1), (0, 2), (1, 1), (1, 2), (2, 2)]):
                for v in range(2):
                    x = jnp.where(is_t[lo_t], d[hi_t][v], 0.0)
                    if lo_t != hi_t:
                        x = jnp.where(is_t[hi_t], d[lo_t][v], x)
                    out_ref[0, a, pl.ds(pl.multiple_of(i0, 16), 16), p * K + v * 128:p * K + (v + 1) * 128] = x.astype(jnp.bfloat16)
        return carry
    lax.fori_loop(0, beads // 16, unfold, 0)

def design(off, mask, rows, kind, cols, by_blocks, unroll=16):
    nb, slots = off.shape
    beads = rows.shape[-1]
    n_src = rows.shape[0]
    return pl.pallas_call(
        functools.partial(design_kernel, by_blocks=by_blocks, beads=beads, slots=slots, unroll=unroll),
        grid_spec=pltpu.PrefetchScalarGridSpec(
            num_scalar_prefetch=2, grid=(nb,),
            in_specs=[
                pl.BlockSpec((n_src, 3, beads), lambda b, *_: (0, 0, 0)),
                pl.BlockSpec((n_src, 1, beads), lambda b, *_: (0, 0, 0)),
                pl.BlockSpec((1, beads, 4), lambda b, *_: (b, 0, 0)),
            ],
            out_specs=pl.BlockSpec((1, 3, beads, PAIRS * K), lambda b, *_: (b, 0, 0, 0)),
            scratch_shapes=[
                pltpu.VMEM((slots, beads, beads), jnp.float32),
                pltpu.VMEM((slots, beads, beads), jnp.float32),
                pltpu.VMEM((slots, beads, beads), jnp.float32),
                pltpu.VMEM((3, slots, beads, beads), jnp.float32),
                pltpu.VMEM((beads * 72, 128), jnp.float32),
                pltpu.SMEM((slots + 1,), jnp.int32),
            ]),
        out_shape=jax.ShapeDtypeStruct((nb, 3, beads, PAIRS * K), jnp.bfloat16),
        compiler_params=pltpu.CompilerParams(vmem_limit_bytes=56 * 1024 * 1024),
    )(off, mask, rows, kind, cols)


def extended(cells, sides, width):
    for axis, dim in sides:
        count = lax.axis_size(axis)
        head = lax.slice_in_dim(cells, 0, width, axis=dim)
        tail = lax.slice_in_dim(cells, cells.shape[dim] - width, cells.shape[dim], axis=dim)
        cells = jnp.concatenate(
            [
                lax.ppermute(tail, axis, [(i, (i + 1) % count) for i in range(count)]),
                cells,
                lax.ppermute(head, axis, [((i + 1) % count, i) for i in range(count)]),
            ],
            axis=dim,
        )
    return cells


def shards(coords, kinds, forces, tile_offsets, tile_mask):
    frames, _, blocks_x, blocks_y, beads = coords.shape
    slots = tile_offsets.shape[3]
    nb = blocks_x * blocks_y
    frame_rows = 3 * beads * nb * lax.axis_size("gx") * lax.axis_size("gy")
    cells = jnp.concatenate(
        [jnp.transpose(coords[0], (1, 2, 0, 3)), kinds.astype(jnp.float32)[:, :, None, :]], axis=2
    )
    around = extended(cells, (("gx", 0), ("gy", 1)), 1)
    around = around.reshape((blocks_x + 2) * (blocks_y + 2), 4, beads)
    cols = jnp.swapaxes(cells.reshape(nb, 4, beads), 1, 2)
    rows = design(
        tile_offsets.reshape(nb, slots),
        tile_mask.reshape(nb, slots),
        around[:, :3],
        around[:, 3:],
        cols,
        blocks_y,
    ).reshape(nb * 3 * beads, PAIRS * K)
    target = jnp.transpose(forces[0], (1, 2, 0, 3)).reshape(nb * 3 * beads)
    gram = lax.dot_general(rows, rows, (((0,), (0,)), ((), ())), preferred_element_type=jnp.float32)
    rhs = jnp.dot(target, rows, preferred_element_type=jnp.float32)
    gram = lax.psum_scatter(gram / frame_rows, "gy", scatter_dimension=0, tiled=True)
    rhs = lax.psum_scatter(rhs / frame_rows, "gy", scatter_dimension=0, tiled=True)
    gram, rhs = lax.psum((gram, rhs), "gx")
    return gram[None], rhs[None]


def solution(mesh):
    placed = (
        P(None, None, "gx", "gy", None),
        P("gx", "gy", None),
        P(None, None, "gx", "gy", None),
        P(None, "gx", "gy", None),
        P(None, "gx", "gy", None),
    )
    return jax.shard_map(
        shards,
        mesh=mesh,
        in_specs=placed,
        out_specs=(P(None, "gy", None), P(None, "gy")),
        check_vma=False,
    )
```

```python
import functools
import math
import jax
import jax.numpy as jnp
import numpy as np
from jax import lax
from jax.experimental import pallas as pl
from jax.experimental.pallas import tpu as pltpu
from jax.sharding import PartitionSpec as P

K=256; PAIRS=6
STEP=32; SPAN=64
ROOT=math.sqrt(0.5*math.log2(math.e))
NEG=-1e9

CLASSES = ((0, 0), (0, 1), (0, 2), (1, 1), (1, 2), (2, 2))
HALF = 128
TILES = PAIRS * K // HALF
CHUNKS = 2
RHS = (-1, -1)


def stored(r, c):
    p, q = CLASSES[r * HALF // K], CLASSES[c * HALF // K]
    return r <= c and bool(set(p) & set(q))


class Plan:
    def __init__(self, size_x, size_y):
        self.size_x = size_x
        self.pairs = size_y // 2
        self.rows = PAIRS * K // size_y
        self.part = HALF // 2 // size_x
        pairs = range(self.pairs)
        tiles = [(r, c) for r in range(TILES) for c in range(TILES) if stored(r, c)]
        needs = {RHS: set(pairs)}
        for r, c in tiles:
            span = [(x * HALF, x * HALF + HALF) for x in (r, c)]
            needs[(r, c)] = {
                g for g in pairs for lo, hi in span
                if lo < (g + 1) * 2 * self.rows and hi > g * 2 * self.rows
            }
        self.slots = -(-(len(tiles) + 1) // (self.pairs * CHUNKS))
        room = self.slots * CHUNKS
        owned = [[] for _ in pairs]
        for tile in sorted(tiles, key=lambda t: len(needs[t])) + [RHS]:
            free = [g for g in pairs if len(owned[g]) < room]
            wanted = [g for g in free if g in needs[tile]] or free
            owned[min(wanted, key=lambda g: len(owned[g]))].append(tile)
        self.owned = owned
        self.place = {t: (g, s) for g in pairs for s, t in enumerate(owned[g])}
        lists = {
            (g, k): [s for s, t in enumerate(owned[g]) if (g ^ k) in needs[t]]
            for g in pairs for k in range(1, self.pairs)
        }
        self.counts = [max(1, max(len(lists[g, k]) for g in pairs)) for k in range(1, self.pairs)]
        self.room = room
        self.send = np.zeros((self.pairs, sum(self.counts)), np.int32)
        self.entries = room + sum(self.counts)
        found = []
        for g in pairs:
            where = {t: s for s, t in enumerate(owned[g])}
            at = 0
            for k in range(1, self.pairs):
                chosen = lists[g, k]
                self.send[g, at:at + len(chosen)] = chosen
                for j, s in enumerate(lists[g ^ k, k]):
                    where[owned[g ^ k][s]] = room + at + j
                at += self.counts[k - 1]
            found.append(where)
        self.unit = math.gcd(self.rows, HALF)
        units = self.rows // self.unit
        self.table = np.zeros((size_y, units * TILES), np.int32)
        self.rhs = np.zeros((size_y,), np.int32)
        for d in range(size_y):
            where = found[d // 2]
            self.rhs[d] = where[RHS]
            for u in range(units):
                r = (d * self.rows + u * self.unit) // HALF
                for c in range(TILES):
                    if stored(r, c):
                        self.table[d, u * TILES + c] = 2 * where[(r, c)]
                    elif stored(c, r):
                        self.table[d, u * TILES + c] = 2 * where[(c, r)] + 1
                    else:
                        self.table[d, u * TILES + c] = -1


def gram_tiles(me_ref, force_ref, rows_s, left_s, outs, plan):
    def put(tile, value):
        g, s = plan.place[tile]
        out = outs[s // plan.slots]
        for h in range(2):
            for z in range(plan.size_x):
                at = h * HALF // 2 + z * plan.part
                out[h ^ me_ref[0], g ^ me_ref[1], z ^ me_ref[2], s % plan.slots] = value[at:at + plan.part]

    used = {(g, s) for g, s in plan.place.values()}
    for g in range(plan.pairs):
        for s in range(plan.room):
            if (g, s) not in used:
                plan_tile = jnp.zeros((plan.part, HALF), jnp.float32)
                for h in range(2):
                    for z in range(plan.size_x):
                        outs[s // plan.slots][h ^ me_ref[0], g ^ me_ref[1], z ^ me_ref[2], s % plan.slots] = plan_tile
    for p in range(PAIRS):
        left_s[...] = rows_s[:, p * K:(p + 1) * K].T
        for q in range(p, PAIRS):
            if not stored(2 * p, 2 * q):
                continue
            block = jnp.dot(left_s[...], rows_s[:, q * K:(q + 1) * K], preferred_element_type=jnp.float32)
            for r in range(2):
                for c in range(2):
                    if stored(2 * p + r, 2 * q + c):
                        put((2 * p + r, 2 * q + c), block[r * HALF:(r + 1) * HALF, c * HALF:(c + 1) * HALF])
    rhs = jnp.dot(force_ref[...], rows_s[...], preferred_element_type=jnp.float32)
    lines = [rhs[0:1, t * HALF:(t + 1) * HALF] for t in range(TILES)]
    put(RHS, jnp.concatenate(lines + [jnp.zeros((HALF - TILES, HALF), jnp.float32)], axis=0))


def design_kernel(off_ref, mask_ref, me_ref, rows_ref, kind_ref, col_ref, force_ref, *refs, plan, by_blocks, beads, slots, unroll):
    outs = refs[:CHUNKS]
    pos_s, lt_s, code_s, w_s, res_s, rows_s, left_s, list_s = refs[CHUNKS:]
    b = pl.program_id(0)
    bx = b // by_blocks
    by = b % by_blocks
    live = jnp.int32(0)
    for t in range(slots):
        list_s[live] = off_ref[b, t]
        live = live + mask_ref[b, t]
    chunks = (live + 1) // 2
    colv = [jnp.broadcast_to(col_ref[0, :, a:a+1], (beads, beads)) for a in range(3)]
    def geom(s, c):
        o = list_s[s]
        ox = o // 3
        oy = o % 3
        src = (bx + ox) * (by_blocks + 2) + by + oy
        sx = (ox - 1).astype(jnp.float32)
        sy = (oy - 1).astype(jnp.float32)
        d0 = colv[0] - rows_ref[src, 0:1, :] - sx
        d1 = colv[1] - rows_ref[src, 1:2, :] - sy
        d2 = colv[2] - rows_ref[src, 2:3, :]
        r2 = d0 * d0 + d1 * d1 + d2 * d2
        u = jnp.sqrt(r2) * K
        m = jnp.minimum(jnp.floor(u * (1.0 / STEP)), K // STEP - 1.0)
        pos_s[s] = (u - m * STEP) * ROOT
        t = jnp.maximum(1.0 - r2, 0.0)
        lt_s[s] = jnp.where(t > 0.0, 2.0 * jnp.log2(jnp.where(t > 0.0, t, 1.0)), NEG)
        code_s[s] = kind_ref[src, 0:1, :] * 8.0 + m
        sc = 1.0 / jnp.sqrt(r2 + 0.05)
        w_s[0, s] = d0 * sc
        w_s[1, s] = d1 * sc
        w_s[2, s] = d2 * sc
        return c
    lax.fori_loop(0, live, geom, 0)
    @pl.when(live % 2 == 1)
    def _():
        z = jnp.zeros((beads, beads), jnp.float32)
        pos_s[live] = z
        lt_s[live] = z + NEG
        code_s[live] = z
        for a in range(3):
            w_s[a, live] = z

    cen = (lax.broadcasted_iota(jnp.int32, (SPAN, beads), 0).astype(jnp.float32) - 15.5) * ROOT
    row24 = lax.broadcasted_iota(jnp.int32, (24, beads), 0).astype(jnp.float32)

    def one(i, n):
        gs = []
        ws = []
        for s in range(n):
            x = pos_s[s, pl.ds(i, 1), :] - cen
            g = jnp.exp2(lt_s[s, pl.ds(i, 1), :] - x * x).astype(jnp.bfloat16)
            gs.append(g)
            hit = code_s[s, pl.ds(i, 1), :] == row24
            w = [jnp.where(hit, w_s[a, s, pl.ds(i, 1), :], 0.0) for a in range(3)]
            ws.append(jnp.concatenate(w, axis=0).astype(jnp.bfloat16))
        g = jnp.concatenate(gs, axis=1)
        w = jnp.concatenate(ws, axis=1)
        r = lax.dot_general(w, g, (((1,), (1,)), ((), ())), preferred_element_type=jnp.float32)
        res_s[pl.ds(pl.multiple_of(i * 72, 8), 72), 0:SPAN] = r

    for c in range(1, slots // 2 + 1):
        @pl.when(chunks == c)
        def _(c=c):
            def body(i, carry):
                for q in range(unroll):
                    one(i * unroll + q, 2 * c)
                return carry
            lax.fori_loop(0, beads // unroll, body, 0)
    @pl.when(chunks == 0)
    def _():
        res_s[...] = jnp.zeros_like(res_s)

    lane = lax.broadcasted_iota(jnp.int32, (8, 128), 1)
    low64 = lane < 64
    def unfold(g, carry):
        i0 = g * 16
        kt16 = jnp.broadcast_to(col_ref[0, pl.ds(pl.multiple_of(i0, 16), 16), 3:4], (16, 128))
        for a in range(3):
            d = []
            for t in range(3):
                halves = []
                for h in range(2):
                    rr = [res_s[pl.ds((i0 + h * 8) * 72 + a * 24 + t * 8 + m, 8, stride=72), :] for m in range(8)]
                    pair = lambda p, q: jnp.where(low64, p, pltpu.roll(q, 64, 1))
                    e0, e1 = pair(rr[0], rr[2]), pair(rr[4], rr[6])
                    o0, o1 = pair(rr[1], rr[3]), pair(rr[5], rr[7])
                    e0, e1 = pltpu.roll(e0, 112, 1), pltpu.roll(e1, 112, 1)
                    o0, o1 = pltpu.roll(o0, 16, 1), pltpu.roll(o1, 16, 1)
                    lo = jnp.where(lane < 112, e0, e1) + jnp.where(lane < 16, 0.0, o0)
                    hi = jnp.where(lane < 112, e1, 0.0) + jnp.where(lane < 16, o0, o1)
                    halves.append((lo, hi))
                d.append([jnp.concatenate([halves[0][v], halves[1][v]], axis=0) for v in range(2)])
            is_t = [kt16 == float(t) for t in range(3)]
            for p, (lo_t, hi_t) in enumerate([(0, 0), (0, 1), (0, 2), (1, 1), (1, 2), (2, 2)]):
                for v in range(2):
                    x = jnp.where(is_t[lo_t], d[hi_t][v], 0.0)
                    if lo_t != hi_t:
                        x = jnp.where(is_t[hi_t], d[lo_t][v], x)
                    rows_s[pl.ds(pl.multiple_of((b * 3 + a) * beads + i0, 16), 16), p * K + v * 128:p * K + (v + 1) * 128] = x.astype(jnp.bfloat16)
        return carry
    lax.fori_loop(0, beads // 16, unfold, 0)

    @pl.when(b == pl.num_programs(0) - 1)
    def _():
        gram_tiles(me_ref, force_ref, rows_s, left_s, outs, plan)


def design(off, mask, me, rows, kind, cols, force, plan, by_blocks, unroll=16):
    nb, slots = off.shape
    beads = rows.shape[-1]
    n_src = rows.shape[0]
    total = nb * 3 * beads
    share = (2, plan.pairs, plan.size_x, plan.slots, plan.part, HALF)
    return pl.pallas_call(
        functools.partial(design_kernel, plan=plan, by_blocks=by_blocks, beads=beads, slots=slots, unroll=unroll),
        grid_spec=pltpu.PrefetchScalarGridSpec(
            num_scalar_prefetch=3,
            grid=(nb,),
            in_specs=[
                pl.BlockSpec((n_src, 3, beads), lambda b, *_: (0, 0, 0)),
                pl.BlockSpec((n_src, 1, beads), lambda b, *_: (0, 0, 0)),
                pl.BlockSpec((1, beads, 4), lambda b, *_: (b, 0, 0)),
                pl.BlockSpec((16, total), lambda b, *_: (0, 0)),
            ],
            out_specs=[pl.BlockSpec(share, lambda b, *_: (0,) * 6)] * CHUNKS,
            scratch_shapes=[
                pltpu.VMEM((slots, beads, beads), jnp.float32),
                pltpu.VMEM((slots, beads, beads), jnp.float32),
                pltpu.VMEM((slots, beads, beads), jnp.float32),
                pltpu.VMEM((3, slots, beads, beads), jnp.float32),
                pltpu.VMEM((beads * 72, 128), jnp.float32),
                pltpu.VMEM((total, PAIRS * K), jnp.bfloat16),
                pltpu.VMEM((K, total), jnp.bfloat16),
                pltpu.SMEM((slots + 1,), jnp.int32),
            ],
        ),
        out_shape=[jax.ShapeDtypeStruct(share, jnp.float32)] * CHUNKS,
        compiler_params=pltpu.CompilerParams(vmem_limit_bytes=56 * 1024 * 1024),
    )(off, mask, me, rows, kind, cols, force)


def pack_kernel(me_ref, send_ref, parts_ref, own_ref, *msg_refs, plan, scale):
    def fetch(ref, j, s):
        for z in range(plan.size_x):
            value = parts_ref[s // plan.slots, z ^ me_ref[2], s % plan.slots]
            ref[j, z * plan.part:(z + 1) * plan.part, :] = value * scale

    for s in range(plan.room):
        fetch(own_ref, s, s)
    at = 0
    for ref, count in zip(msg_refs, plan.counts):
        for j in range(count):
            fetch(ref, j, send_ref[me_ref[1], at + j])
        at += count


def pack(me, parts, plan, scale):
    shapes = [(n, HALF // 2, HALF) for n in [plan.room] + plan.counts]
    return pl.pallas_call(
        functools.partial(pack_kernel, plan=plan, scale=scale),
        grid_spec=pltpu.PrefetchScalarGridSpec(
            num_scalar_prefetch=2,
            grid=(1,),
            in_specs=[pl.BlockSpec(parts.shape, lambda b, *_: (0,) * parts.ndim)],
            out_specs=[pl.BlockSpec(s, lambda b, *_: (0, 0, 0)) for s in shapes],
        ),
        out_shape=[jax.ShapeDtypeStruct(s, jnp.float32) for s in shapes],
        compiler_params=pltpu.CompilerParams(vmem_limit_bytes=32 * 1024 * 1024),
    )(me, jnp.asarray(plan.send), parts)


def place_kernel(me_ref, table_ref, rhs_at_ref, mine_ref, other_ref, gram_ref, rhs_ref, full_s, *, plan):
    half = HALF // 2
    core = me_ref[0]
    dev = me_ref[3]
    full_s[:, pl.ds(pl.multiple_of(core * half, half), half), :] = mine_ref[...]
    full_s[:, pl.ds(pl.multiple_of((1 - core) * half, half), half), :] = other_ref[...]
    for u in range(plan.rows // plan.unit):
        at = (dev * plan.rows + u * plan.unit) % HALF
        for c in range(TILES):
            entry = table_ref[dev, u * TILES + c]
            cut = (slice(u * plan.unit, (u + 1) * plan.unit), slice(c * HALF, (c + 1) * HALF))

            @pl.when(entry < 0)
            def _(cut=cut):
                gram_ref[cut] = jnp.zeros((plan.unit, HALF), jnp.float32)

            @pl.when(jnp.logical_and(entry >= 0, entry % 2 == 0))
            def _(cut=cut, entry=entry, at=at):
                gram_ref[cut] = full_s[entry // 2, pl.ds(pl.multiple_of(at, plan.unit), plan.unit), :]

            @pl.when(jnp.logical_and(entry >= 0, entry % 2 == 1))
            def _(cut=cut, entry=entry, at=at):
                turned = full_s[entry // 2].T
                value = turned[0:plan.unit]
                for v in range(1, HALF // plan.unit):
                    value = jnp.where(at == v * plan.unit, turned[v * plan.unit:(v + 1) * plan.unit], value)
                gram_ref[cut] = value
    rhs_ref[...] = full_s[rhs_at_ref[dev], 0:16, :]


def place(me, mine, other, plan):
    return pl.pallas_call(
        functools.partial(place_kernel, plan=plan),
        grid_spec=pltpu.PrefetchScalarGridSpec(
            num_scalar_prefetch=3,
            grid=(1,),
            in_specs=[pl.BlockSpec(mine.shape, lambda b, *_: (0, 0, 0))] * 2,
            out_specs=[
                pl.BlockSpec((plan.rows, PAIRS * K), lambda b, *_: (0, 0)),
                pl.BlockSpec((16, HALF), lambda b, *_: (0, 0)),
            ],
            scratch_shapes=[pltpu.VMEM((plan.entries, HALF, HALF), jnp.float32)],
        ),
        out_shape=[
            jax.ShapeDtypeStruct((plan.rows, PAIRS * K), jnp.float32),
            jax.ShapeDtypeStruct((16, HALF), jnp.float32),
        ],
        compiler_params=pltpu.CompilerParams(vmem_limit_bytes=32 * 1024 * 1024),
    )(me, jnp.asarray(plan.table), jnp.asarray(plan.rhs), mine, other)


def extended(cells, sides, width):
    for axis, dim in sides:
        count = lax.axis_size(axis)
        head = lax.slice_in_dim(cells, 0, width, axis=dim)
        tail = lax.slice_in_dim(cells, cells.shape[dim] - width, cells.shape[dim], axis=dim)
        cells = jnp.concatenate(
            [
                lax.ppermute(tail, axis, [(i, (i + 1) % count) for i in range(count)]),
                cells,
                lax.ppermute(head, axis, [((i + 1) % count, i) for i in range(count)]),
            ],
            axis=dim,
        )
    return cells


def swap(x, axis, flip):
    return lax.ppermute(x, axis, [(i, i ^ flip) for i in range(lax.axis_size(axis))])


def summed(x, plan):
    x = x[0] + swap(x[1], "gy", 1)
    got = [swap(x[k], "gy", 2 * k) for k in range(1, plan.pairs)]
    x = functools.reduce(jnp.add, got, x[0])
    got = [swap(x[k], "gx", k) for k in range(1, plan.size_x)]
    x = functools.reduce(jnp.add, got, x[0])
    return jnp.stack([x] + [swap(x, "gx", k) for k in range(1, plan.size_x)])


def shards(coords, kinds, forces, tile_offsets, tile_mask):
    frames, _, blocks_x, blocks_y, beads = coords.shape
    slots = tile_offsets.shape[3]
    nb = blocks_x * blocks_y
    size_x, size_y = lax.axis_size("gx"), lax.axis_size("gy")
    frame_rows = 3 * beads * nb * size_x * size_y
    plan = Plan(size_x, size_y)
    dev = lax.axis_index("gy")
    me = jnp.stack([dev % 2, dev // 2, lax.axis_index("gx"), dev]).astype(jnp.int32)
    cells = jnp.concatenate(
        [jnp.transpose(coords[0], (1, 2, 0, 3)), kinds.astype(jnp.float32)[:, :, None, :]], axis=2
    )
    around = extended(cells, (("gx", 0), ("gy", 1)), 1)
    around = around.reshape((blocks_x + 2) * (blocks_y + 2), 4, beads)
    cols = jnp.swapaxes(cells.reshape(nb, 4, beads), 1, 2)
    force = jnp.transpose(forces[0], (1, 2, 0, 3)).reshape(1, nb * 3 * beads)
    chunks = design(
        tile_offsets.reshape(nb, slots),
        tile_mask.reshape(nb, slots),
        me,
        around[:, :3],
        around[:, 3:],
        cols,
        jnp.broadcast_to(force, (16, nb * 3 * beads)),
        plan,
        blocks_y,
    )
    parts = jnp.stack([summed(x, plan) for x in chunks])
    own, *messages = pack(me, parts, plan, 1.0 / frame_rows)
    got = [swap(m, "gy", 2 * k) for k, m in enumerate(messages, 1)]
    mine = jnp.concatenate([own] + got)
    gram, lines = place(me, mine, swap(mine, "gy", 1), plan)
    rhs = lax.dynamic_slice(lines.reshape(16 * HALF), (dev * plan.rows,), (plan.rows,))
    return gram[None], rhs[None]


def solution(mesh):
    placed = (
        P(None, None, "gx", "gy", None),
        P("gx", "gy", None),
        P(None, None, "gx", "gy", None),
        P(None, "gx", "gy", None),
        P(None, "gx", "gy", None),
    )
    return jax.shard_map(
        shards,
        mesh=mesh,
        in_specs=placed,
        out_specs=(P(None, "gy", None), P(None, "gy")),
        check_vma=False,
    )
```

```python
import functools
import math
import jax
import jax.numpy as jnp
import numpy as np
from jax import lax
from jax.experimental import pallas as pl
from jax.experimental.pallas import tpu as pltpu
from jax.sharding import PartitionSpec as P

K=256; PAIRS=6
STEP=32; SPAN=64
ROOT=math.sqrt(0.5*math.log2(math.e))
NEG=-1e9

CLASSES = ((0, 0), (0, 1), (0, 2), (1, 1), (1, 2), (2, 2))
HALF = 128
TILES = PAIRS * K // HALF
CHUNKS = 2
RHS = (-1, -1)


def stored(r, c):
    p, q = CLASSES[r * HALF // K], CLASSES[c * HALF // K]
    return r <= c and bool(set(p) & set(q))


class Plan:
    def __init__(self, size_x, size_y):
        self.size_x = size_x
        self.pairs = size_y // 2
        self.rows = PAIRS * K // size_y
        self.part = HALF // 2 // size_x
        pairs = range(self.pairs)
        tiles = [(r, c) for r in range(TILES) for c in range(TILES) if stored(r, c)]
        needs = {RHS: set(pairs)}
        for r, c in tiles:
            span = [(x * HALF, x * HALF + HALF) for x in (r, c)]
            needs[(r, c)] = {
                g for g in pairs for lo, hi in span
                if lo < (g + 1) * 2 * self.rows and hi > g * 2 * self.rows
            }
        self.slots = -(-(len(tiles) + 1) // (self.pairs * CHUNKS))
        room = self.slots * CHUNKS
        owned = [[] for _ in pairs]
        for tile in sorted(tiles, key=lambda t: len(needs[t])) + [RHS]:
            free = [g for g in pairs if len(owned[g]) < room]
            wanted = [g for g in free if g in needs[tile]] or free
            owned[min(wanted, key=lambda g: len(owned[g]))].append(tile)
        self.owned = owned
        self.place = {t: (g, s) for g in pairs for s, t in enumerate(owned[g])}
        lists = {
            (g, k): [s for s, t in enumerate(owned[g]) if (g ^ k) in needs[t]]
            for g in pairs for k in range(1, self.pairs)
        }
        self.counts = [max(1, max(len(lists[g, k]) for g in pairs)) for k in range(1, self.pairs)]
        self.room = room
        self.send = np.zeros((self.pairs, sum(self.counts)), np.int32)
        self.entries = room + sum(self.counts)
        found = []
        for g in pairs:
            where = {t: s for s, t in enumerate(owned[g])}
            at = 0
            for k in range(1, self.pairs):
                chosen = lists[g, k]
                self.send[g, at:at + len(chosen)] = chosen
                for j, s in enumerate(lists[g ^ k, k]):
                    where[owned[g ^ k][s]] = room + at + j
                at += self.counts[k - 1]
            found.append(where)
        self.unit = math.gcd(self.rows, HALF)
        units = self.rows // self.unit
        self.table = np.zeros((size_y, units * TILES), np.int32)
        self.rhs = np.zeros((size_y,), np.int32)
        for d in range(size_y):
            where = found[d // 2]
            self.rhs[d] = where[RHS]
            for u in range(units):
                r = (d * self.rows + u * self.unit) // HALF
                for c in range(TILES):
                    if stored(r, c):
                        self.table[d, u * TILES + c] = 2 * where[(r, c)]
                    elif stored(c, r):
                        self.table[d, u * TILES + c] = 2 * where[(c, r)] + 1
                    else:
                        self.table[d, u * TILES + c] = -1


def gram_tiles(me_ref, force_ref, rows_s, left_s, outs, plan):
    def put(tile, value):
        g, s = plan.place[tile]
        out = outs[s // plan.slots]
        for h in range(2):
            for z in range(plan.size_x):
                at = h * HALF // 2 + z * plan.part
                out[h ^ me_ref[0], g ^ me_ref[1], z ^ me_ref[2], s % plan.slots] = value[at:at + plan.part]

    used = {(g, s) for g, s in plan.place.values()}
    for g in range(plan.pairs):
        for s in range(plan.room):
            if (g, s) not in used:
                plan_tile = jnp.zeros((plan.part, HALF), jnp.float32)
                for h in range(2):
                    for z in range(plan.size_x):
                        outs[s // plan.slots][h ^ me_ref[0], g ^ me_ref[1], z ^ me_ref[2], s % plan.slots] = plan_tile
    for p in range(PAIRS):
        left_s[...] = rows_s[:, p * K:(p + 1) * K].T
        for q in range(p, PAIRS):
            if not stored(2 * p, 2 * q):
                continue
            block = jnp.dot(left_s[...], rows_s[:, q * K:(q + 1) * K], preferred_element_type=jnp.float32)
            for r in range(2):
                for c in range(2):
                    if stored(2 * p + r, 2 * q + c):
                        put((2 * p + r, 2 * q + c), block[r * HALF:(r + 1) * HALF, c * HALF:(c + 1) * HALF])
    rhs = jnp.dot(force_ref[...], rows_s[...], preferred_element_type=jnp.float32)
    lines = [rhs[0:1, t * HALF:(t + 1) * HALF] for t in range(TILES)]
    put(RHS, jnp.concatenate(lines + [jnp.zeros((HALF - TILES, HALF), jnp.float32)], axis=0))


def design_kernel(off_ref, mask_ref, me_ref, rows_ref, kind_ref, col_ref, force_ref, *refs, plan, by_blocks, beads, slots, groups):
    outs = refs[:CHUNKS]
    pos_s, lt_s, code_s, w_s, res_s, rows_s, left_s, list_s = refs[CHUNKS:]
    b = pl.program_id(0)
    bx = b // by_blocks
    by = b % by_blocks
    live = jnp.int32(0)
    for t in range(slots):
        list_s[live] = off_ref[b, t]
        live = live + mask_ref[b, t]
    colv = [jnp.broadcast_to(col_ref[0, :, a:a+1], (beads, beads)) for a in range(3)]
    def geom(s, c):
        o = list_s[s]
        ox = o // 3
        oy = o % 3
        src = (bx + ox) * (by_blocks + 2) + by + oy
        sx = (ox - 1).astype(jnp.float32)
        sy = (oy - 1).astype(jnp.float32)
        d0 = colv[0] - rows_ref[src, 0:1, :] - sx
        d1 = colv[1] - rows_ref[src, 1:2, :] - sy
        d2 = colv[2] - rows_ref[src, 2:3, :]
        r2 = d0 * d0 + d1 * d1 + d2 * d2
        u = jnp.sqrt(r2) * K
        m = jnp.minimum(jnp.floor(u * (1.0 / STEP)), K // STEP - 1.0)
        pos_s[s] = (u - m * STEP) * ROOT
        t = jnp.maximum(1.0 - r2, 0.0)
        lt_s[s] = jnp.where(t > 0.0, 2.0 * jnp.log2(jnp.where(t > 0.0, t, 1.0)), NEG)
        code_s[s] = kind_ref[src, 0:1, :] * 8.0 + m
        sc = 1.0 / jnp.sqrt(r2 + 0.05)
        w_s[0, s] = d0 * sc
        w_s[1, s] = d1 * sc
        w_s[2, s] = d2 * sc
        return c
    lax.fori_loop(0, live, geom, 0)
    first = (lax.broadcasted_iota(jnp.int32, (8, beads), 0).astype(jnp.float32) - 15.5) * ROOT
    row24 = lax.broadcasted_iota(jnp.int32, (24, beads), 0).astype(jnp.float32)
    lane = lax.broadcasted_iota(jnp.int32, (8, 128), 1)
    low = lane < 64
    ahead = 8.0 * ROOT

    def factors(i, s):
        x = pos_s[s, pl.ds(i, 1), :] - first
        e = lt_s[s, pl.ds(i, 1), :] - x * x
        d = x * (2.0 * ahead) - ahead * ahead
        powers = [e]
        for v in range(1, SPAN // 8):
            e = e + d
            d = d - 2.0 * ahead * ahead
            powers.append(e)
        g = jnp.exp2(jnp.concatenate(powers[2:] + powers[:2], axis=0)).astype(jnp.bfloat16)
        hit = code_s[s, pl.ds(i, 1), :] == row24
        w = [jnp.where(hit, w_s[a, s, pl.ds(i, 1), :], 0.0) for a in range(3)]
        return g, jnp.concatenate(w, axis=0).astype(jnp.bfloat16)

    def couple(i, at, n):
        both = [[factors(i + 8 * k, s) for s in range(n)] for k in range(2)]
        g = jnp.concatenate([jnp.concatenate([f[0] for f in row], axis=1) for row in both], axis=0)
        w = jnp.concatenate([jnp.concatenate([f[1] for f in row], axis=1) for row in both], axis=0)
        r = lax.dot_general(w, g, (((1,), (1,)), ((), ())), preferred_element_type=jnp.float32)
        left = lax.broadcasted_iota(jnp.int32, (72, 128), 1) < 64
        res_s[pl.ds(pl.multiple_of(at * 72, 8), 72), :] = jnp.where(left, r[0:72], r[72:144])

    for n in range(1, slots + 1):
        @pl.when(live == n)
        def _(n=n):
            def body(g, carry):
                for q in range(8 * groups):
                    couple((g * groups + q // 8) * 16 + q % 8, (g * groups + q // 8) * 8 + q % 8, n)
                return carry
            lax.fori_loop(0, beads // (16 * groups), body, 0)

    @pl.when(live == 0)
    def _():
        res_s[...] = jnp.zeros_like(res_s)

    cut = lane % 64

    def unfold(g, carry):
        i0 = g * 16
        kt16 = jnp.broadcast_to(col_ref[0, pl.ds(pl.multiple_of(i0, 16), 16), 3:4], (16, 128))
        is_t = [kt16 == float(t) for t in range(3)]
        for a in range(3):
            d = []
            for t in range(3):
                r = [res_s[pl.ds(g * 8 * 72 + a * 24 + t * 8 + m, 8, stride=72), :] for m in range(8)]
                r = [jnp.zeros_like(lane, jnp.float32)] + r + [jnp.zeros_like(lane, jnp.float32)]
                halves = []
                for v in range(2):
                    m = 4 * v + 1
                    el = jnp.where(cut < 48, r[m], r[m + 2])
                    eu = jnp.where(cut < 48, r[m + 2], r[min(m + 4, 9)])
                    ol = jnp.where(cut < 48, r[m + 1], r[m + 3])
                    ou = jnp.where(cut < 32, r[m + 3], jnp.where(cut < 48, r[m - 1], r[m + 1]))
                    et = pltpu.roll(jnp.where(low, eu, el), 64, 1)
                    ot = pltpu.roll(jnp.where(low, ou, ol), 64, 1)
                    near = jnp.where(low, el, et) + pltpu.roll(jnp.where(low, ol, ot), 32, 1)
                    far = jnp.where(low, et, eu) + pltpu.roll(jnp.where(low, ot, ou), 32, 1)
                    halves.append(jnp.concatenate([near, far], axis=0))
                d.append(halves)
            for p, (lo_t, hi_t) in enumerate(CLASSES):
                for v in range(2):
                    x = jnp.where(is_t[lo_t], d[hi_t][v], 0.0)
                    if lo_t != hi_t:
                        x = jnp.where(is_t[hi_t], d[lo_t][v], x)
                    rows_s[pl.ds(pl.multiple_of((b * 3 + a) * beads + i0, 16), 16), p * K + v * 128:p * K + (v + 1) * 128] = x.astype(jnp.bfloat16)
        return carry
    lax.fori_loop(0, beads // 16, unfold, 0)

    @pl.when(b == pl.num_programs(0) - 1)
    def _():
        gram_tiles(me_ref, force_ref, rows_s, left_s, outs, plan)


def design(off, mask, me, rows, kind, cols, force, plan, by_blocks, groups=2):
    nb, slots = off.shape
    beads = rows.shape[-1]
    n_src = rows.shape[0]
    total = nb * 3 * beads
    share = (2, plan.pairs, plan.size_x, plan.slots, plan.part, HALF)
    return pl.pallas_call(
        functools.partial(design_kernel, plan=plan, by_blocks=by_blocks, beads=beads, slots=slots, groups=groups),
        grid_spec=pltpu.PrefetchScalarGridSpec(
            num_scalar_prefetch=3,
            grid=(nb,),
            in_specs=[
                pl.BlockSpec((n_src, 3, beads), lambda b, *_: (0, 0, 0)),
                pl.BlockSpec((n_src, 1, beads), lambda b, *_: (0, 0, 0)),
                pl.BlockSpec((1, beads, 4), lambda b, *_: (b, 0, 0)),
                pl.BlockSpec((16, total), lambda b, *_: (0, 0)),
            ],
            out_specs=[pl.BlockSpec(share, lambda b, *_: (0,) * 6)] * CHUNKS,
            scratch_shapes=[
                pltpu.VMEM((slots, beads, beads), jnp.float32),
                pltpu.VMEM((slots, beads, beads), jnp.float32),
                pltpu.VMEM((slots, beads, beads), jnp.float32),
                pltpu.VMEM((3, slots, beads, beads), jnp.float32),
                pltpu.VMEM((beads // 2 * 72, 128), jnp.float32),
                pltpu.VMEM((total, PAIRS * K), jnp.bfloat16),
                pltpu.VMEM((K, total), jnp.bfloat16),
                pltpu.SMEM((slots + 1,), jnp.int32),
            ],
        ),
        out_shape=[jax.ShapeDtypeStruct(share, jnp.float32)] * CHUNKS,
        compiler_params=pltpu.CompilerParams(vmem_limit_bytes=56 * 1024 * 1024),
    )(off, mask, me, rows, kind, cols, force)


def pack_kernel(me_ref, send_ref, parts_ref, own_ref, *msg_refs, plan, scale):
    def fetch(ref, j, s):
        for z in range(plan.size_x):
            value = parts_ref[s // plan.slots, z ^ me_ref[2], s % plan.slots]
            ref[j, z * plan.part:(z + 1) * plan.part, :] = value * scale

    for s in range(plan.room):
        fetch(own_ref, s, s)
    at = 0
    for ref, count in zip(msg_refs, plan.counts):
        for j in range(count):
            fetch(ref, j, send_ref[me_ref[1], at + j])
        at += count


def pack(me, parts, plan, scale):
    shapes = [(n, HALF // 2, HALF) for n in [plan.room] + plan.counts]
    return pl.pallas_call(
        functools.partial(pack_kernel, plan=plan, scale=scale),
        grid_spec=pltpu.PrefetchScalarGridSpec(
            num_scalar_prefetch=2,
            grid=(1,),
            in_specs=[pl.BlockSpec(parts.shape, lambda b, *_: (0,) * parts.ndim)],
            out_specs=[pl.BlockSpec(s, lambda b, *_: (0, 0, 0)) for s in shapes],
        ),
        out_shape=[jax.ShapeDtypeStruct(s, jnp.float32) for s in shapes],
        compiler_params=pltpu.CompilerParams(vmem_limit_bytes=32 * 1024 * 1024),
    )(me, jnp.asarray(plan.send), parts)


def place_kernel(me_ref, table_ref, rhs_at_ref, mine_ref, other_ref, gram_ref, rhs_ref, full_s, *, plan):
    half = HALF // 2
    core = me_ref[0]
    dev = me_ref[3]
    full_s[:, pl.ds(pl.multiple_of(core * half, half), half), :] = mine_ref[...]
    full_s[:, pl.ds(pl.multiple_of((1 - core) * half, half), half), :] = other_ref[...]
    for u in range(plan.rows // plan.unit):
        at = (dev * plan.rows + u * plan.unit) % HALF
        for c in range(TILES):
            entry = table_ref[dev, u * TILES + c]
            cut = (slice(u * plan.unit, (u + 1) * plan.unit), slice(c * HALF, (c + 1) * HALF))

            @pl.when(entry < 0)
            def _(cut=cut):
                gram_ref[cut] = jnp.zeros((plan.unit, HALF), jnp.float32)

            @pl.when(jnp.logical_and(entry >= 0, entry % 2 == 0))
            def _(cut=cut, entry=entry, at=at):
                gram_ref[cut] = full_s[entry // 2, pl.ds(pl.multiple_of(at, plan.unit), plan.unit), :]

            @pl.when(jnp.logical_and(entry >= 0, entry % 2 == 1))
            def _(cut=cut, entry=entry, at=at):
                turned = full_s[entry // 2].T
                value = turned[0:plan.unit]
                for v in range(1, HALF // plan.unit):
                    value = jnp.where(at == v * plan.unit, turned[v * plan.unit:(v + 1) * plan.unit], value)
                gram_ref[cut] = value
    rhs_ref[...] = full_s[rhs_at_ref[dev], 0:16, :]


def place(me, mine, other, plan):
    return pl.pallas_call(
        functools.partial(place_kernel, plan=plan),
        grid_spec=pltpu.PrefetchScalarGridSpec(
            num_scalar_prefetch=3,
            grid=(1,),
            in_specs=[pl.BlockSpec(mine.shape, lambda b, *_: (0, 0, 0))] * 2,
            out_specs=[
                pl.BlockSpec((plan.rows, PAIRS * K), lambda b, *_: (0, 0)),
                pl.BlockSpec((16, HALF), lambda b, *_: (0, 0)),
            ],
            scratch_shapes=[pltpu.VMEM((plan.entries, HALF, HALF), jnp.float32)],
        ),
        out_shape=[
            jax.ShapeDtypeStruct((plan.rows, PAIRS * K), jnp.float32),
            jax.ShapeDtypeStruct((16, HALF), jnp.float32),
        ],
        compiler_params=pltpu.CompilerParams(vmem_limit_bytes=32 * 1024 * 1024),
    )(me, jnp.asarray(plan.table), jnp.asarray(plan.rhs), mine, other)


def extended(cells, sides, width):
    for axis, dim in sides:
        count = lax.axis_size(axis)
        head = lax.slice_in_dim(cells, 0, width, axis=dim)
        tail = lax.slice_in_dim(cells, cells.shape[dim] - width, cells.shape[dim], axis=dim)
        cells = jnp.concatenate(
            [
                lax.ppermute(tail, axis, [(i, (i + 1) % count) for i in range(count)]),
                cells,
                lax.ppermute(head, axis, [((i + 1) % count, i) for i in range(count)]),
            ],
            axis=dim,
        )
    return cells


def swap(x, axis, flip):
    return lax.ppermute(x, axis, [(i, i ^ flip) for i in range(lax.axis_size(axis))])


def summed(x, plan):
    x = x[0] + swap(x[1], "gy", 1)
    got = [swap(x[k], "gy", 2 * k) for k in range(1, plan.pairs)]
    x = functools.reduce(jnp.add, got, x[0])
    got = [swap(x[k], "gx", k) for k in range(1, plan.size_x)]
    x = functools.reduce(jnp.add, got, x[0])
    return jnp.stack([x] + [swap(x, "gx", k) for k in range(1, plan.size_x)])


def shards(coords, kinds, forces, tile_offsets, tile_mask):
    frames, _, blocks_x, blocks_y, beads = coords.shape
    slots = tile_offsets.shape[3]
    nb = blocks_x * blocks_y
    size_x, size_y = lax.axis_size("gx"), lax.axis_size("gy")
    frame_rows = 3 * beads * nb * size_x * size_y
    plan = Plan(size_x, size_y)
    dev = lax.axis_index("gy")
    me = jnp.stack([dev % 2, dev // 2, lax.axis_index("gx"), dev]).astype(jnp.int32)
    cells = jnp.concatenate(
        [jnp.transpose(coords[0], (1, 2, 0, 3)), kinds.astype(jnp.float32)[:, :, None, :]], axis=2
    )
    around = extended(cells, (("gx", 0), ("gy", 1)), 1)
    around = around.reshape((blocks_x + 2) * (blocks_y + 2), 4, beads)
    cols = jnp.swapaxes(cells.reshape(nb, 4, beads), 1, 2)
    force = jnp.transpose(forces[0], (1, 2, 0, 3)).reshape(1, nb * 3 * beads)
    chunks = design(
        tile_offsets.reshape(nb, slots),
        tile_mask.reshape(nb, slots),
        me,
        around[:, :3],
        around[:, 3:],
        cols,
        jnp.broadcast_to(force, (16, nb * 3 * beads)),
        plan,
        blocks_y,
    )
    parts = jnp.stack([summed(x, plan) for x in chunks])
    own, *messages = pack(me, parts, plan, 1.0 / frame_rows)
    got = [swap(m, "gy", 2 * k) for k, m in enumerate(messages, 1)]
    mine = jnp.concatenate([own] + got)
    gram, lines = place(me, mine, swap(mine, "gy", 1), plan)
    rhs = lax.dynamic_slice(lines.reshape(16 * HALF), (dev * plan.rows,), (plan.rows,))
    return gram[None], rhs[None]


def solution(mesh):
    placed = (
        P(None, None, "gx", "gy", None),
        P("gx", "gy", None),
        P(None, None, "gx", "gy", None),
        P(None, "gx", "gy", None),
        P(None, "gx", "gy", None),
    )
    return jax.shard_map(
        shards,
        mesh=mesh,
        in_specs=placed,
        out_specs=(P(None, "gy", None), P(None, "gy")),
        check_vma=False,
    )
```

```python
import functools
import math
import jax
import jax.numpy as jnp
import numpy as np
from jax import lax
from jax.experimental import pallas as pl
from jax.experimental.pallas import tpu as pltpu
from jax.sharding import PartitionSpec as P

K=256; PAIRS=6
STEP=32; SPAN=64
ROOT=math.sqrt(0.5*math.log2(math.e))
NEG=-1e9
MID=3

CLASSES = ((0, 0), (0, 1), (0, 2), (1, 1), (1, 2), (2, 2))
HALF = 128
TILES = PAIRS * K // HALF
CHUNKS = 2
RHS = (-1, -1)


def stored(r, c):
    p, q = CLASSES[r * HALF // K], CLASSES[c * HALF // K]
    return r <= c and bool(set(p) & set(q))


class Plan:
    def __init__(self, size_x, size_y):
        self.size_x = size_x
        self.pairs = size_y // 2
        self.rows = PAIRS * K // size_y
        self.part = HALF // 2 // size_x
        pairs = range(self.pairs)
        tiles = [(r, c) for r in range(TILES) for c in range(TILES) if stored(r, c)]
        needs = {RHS: set(pairs)}
        for r, c in tiles:
            span = [(x * HALF, x * HALF + HALF) for x in (r, c)]
            needs[(r, c)] = {
                g for g in pairs for lo, hi in span
                if lo < (g + 1) * 2 * self.rows and hi > g * 2 * self.rows
            }
        self.slots = -(-(len(tiles) + 1) // (self.pairs * CHUNKS))
        room = self.slots * CHUNKS
        owned = [[] for _ in pairs]
        for tile in sorted(tiles, key=lambda t: len(needs[t])) + [RHS]:
            free = [g for g in pairs if len(owned[g]) < room]
            wanted = [g for g in free if g in needs[tile]] or free
            owned[min(wanted, key=lambda g: len(owned[g]))].append(tile)
        self.owned = owned
        self.place = {t: (g, s) for g in pairs for s, t in enumerate(owned[g])}
        lists = {
            (g, k): [s for s, t in enumerate(owned[g]) if (g ^ k) in needs[t]]
            for g in pairs for k in range(1, self.pairs)
        }
        self.counts = [max(1, max(len(lists[g, k]) for g in pairs)) for k in range(1, self.pairs)]
        self.room = room
        self.send = np.zeros((self.pairs, sum(self.counts)), np.int32)
        self.entries = room + sum(self.counts)
        found = []
        for g in pairs:
            where = {t: s for s, t in enumerate(owned[g])}
            at = 0
            for k in range(1, self.pairs):
                chosen = lists[g, k]
                self.send[g, at:at + len(chosen)] = chosen
                for j, s in enumerate(lists[g ^ k, k]):
                    where[owned[g ^ k][s]] = room + at + j
                at += self.counts[k - 1]
            found.append(where)
        self.unit = math.gcd(self.rows, HALF)
        units = self.rows // self.unit
        self.table = np.zeros((size_y, units * TILES), np.int32)
        self.rhs = np.zeros((size_y,), np.int32)
        for d in range(size_y):
            where = found[d // 2]
            self.rhs[d] = where[RHS]
            for u in range(units):
                r = (d * self.rows + u * self.unit) // HALF
                for c in range(TILES):
                    if stored(r, c):
                        self.table[d, u * TILES + c] = 2 * where[(r, c)]
                    elif stored(c, r):
                        self.table[d, u * TILES + c] = 2 * where[(c, r)] + 1
                    else:
                        self.table[d, u * TILES + c] = -1


def gram_tiles(me_ref, force_ref, rows_s, left_s, outs, plan):
    def put(tile, value):
        g, s = plan.place[tile]
        out = outs[s // plan.slots]
        for h in range(2):
            for z in range(plan.size_x):
                at = h * HALF // 2 + z * plan.part
                out[h ^ me_ref[0], g ^ me_ref[1], z ^ me_ref[2], s % plan.slots] = value[at:at + plan.part]

    used = {(g, s) for g, s in plan.place.values()}
    for g in range(plan.pairs):
        for s in range(plan.room):
            if (g, s) not in used:
                plan_tile = jnp.zeros((plan.part, HALF), jnp.float32)
                for h in range(2):
                    for z in range(plan.size_x):
                        outs[s // plan.slots][h ^ me_ref[0], g ^ me_ref[1], z ^ me_ref[2], s % plan.slots] = plan_tile
    for p in range(PAIRS):
        left_s[...] = rows_s[:, p * K:(p + 1) * K].T
        for q in range(p, PAIRS):
            if not stored(2 * p, 2 * q):
                continue
            block = jnp.dot(left_s[...], rows_s[:, q * K:(q + 1) * K], preferred_element_type=jnp.float32)
            for r in range(2):
                for c in range(2):
                    if stored(2 * p + r, 2 * q + c):
                        put((2 * p + r, 2 * q + c), block[r * HALF:(r + 1) * HALF, c * HALF:(c + 1) * HALF])
    rhs = jnp.dot(force_ref[...], rows_s[...], preferred_element_type=jnp.float32)
    lines = [rhs[0:1, t * HALF:(t + 1) * HALF] for t in range(TILES)]
    put(RHS, jnp.concatenate(lines + [jnp.zeros((HALF - TILES, HALF), jnp.float32)], axis=0))


def design_kernel(off_ref, mask_ref, me_ref, strip_ref, below_ref, above_ref, force_ref, *refs, plan, by_blocks, beads, slots, groups):
    outs = refs[:CHUNKS]
    pos_s, lt_s, code_s, w_s, res_s, rows_s, left_s, near_s, col_s, list_s = refs[CHUNKS:]
    b = pl.program_id(0)
    bx = b // by_blocks
    by = b % by_blocks
    live = jnp.int32(0)
    for t in range(slots):
        list_s[live] = off_ref[b, t]
        live = live + mask_ref[b, t]

    @pl.when(b == 0)
    def _():
        near_s[...] = jnp.zeros_like(near_s)
        for x in range(strip_ref.shape[0]):
            near_s[x * (by_blocks + 2), 0:4] = below_ref[x, by_blocks - 1]
            for y in range(by_blocks):
                near_s[x * (by_blocks + 2) + y + 1, 0:4] = strip_ref[x, y]
            near_s[x * (by_blocks + 2) + by_blocks + 1, 0:4] = above_ref[x, 0]

    col_s[...] = near_s[(bx + 1) * (by_blocks + 2) + by + 1].T
    colv = [jnp.broadcast_to(col_s[:, a:a + 1], (beads, beads)) for a in range(3)]

    def geom(s, c):
        o = list_s[s]
        ox = o // 3
        oy = o % 3
        src = (bx + ox) * (by_blocks + 2) + by + oy
        sx = (ox - 1).astype(jnp.float32)
        sy = (oy - 1).astype(jnp.float32)
        d0 = colv[0] - near_s[src, 0:1, :] - sx
        d1 = colv[1] - near_s[src, 1:2, :] - sy
        d2 = colv[2] - near_s[src, 2:3, :]
        r2 = d0 * d0 + d1 * d1 + d2 * d2
        u = jnp.sqrt(r2) * K
        m = jnp.minimum(jnp.floor(u * (1.0 / STEP)), K // STEP - 1.0)
        pos_s[s] = (u - m * STEP) * ROOT
        t = jnp.maximum(1.0 - r2, 0.0)
        lt_s[s] = jnp.where(t > 0.0, 2.0 * jnp.log2(jnp.where(t > 0.0, t, 1.0)), NEG)
        code_s[s] = near_s[src, 3:4, :] * 8.0 + m
        sc = 1.0 / jnp.sqrt(r2 + 0.05)
        w_s[0, s] = d0 * sc
        w_s[1, s] = d1 * sc
        w_s[2, s] = d2 * sc
        return c
    lax.fori_loop(0, live, geom, 0)
    middle = (lax.broadcasted_iota(jnp.int32, (8, beads), 0).astype(jnp.float32) + (8 * MID - 15.5)) * ROOT
    row24 = lax.broadcasted_iota(jnp.int32, (24, beads), 0).astype(jnp.float32)
    lane = lax.broadcasted_iota(jnp.int32, (8, 128), 1)
    low = lane < 64
    ahead = 8.0 * ROOT

    def factors(i, s):
        x = pos_s[s, pl.ds(i, 1), :] - middle
        up = lt_s[s, pl.ds(i, 1), :] - x * x
        down = up
        rise = x * (2.0 * ahead) - ahead * ahead
        fall = rise
        powers = {MID: up}
        for v in range(1, SPAN // 8):
            if MID + v < SPAN // 8:
                up = up + rise
                rise = rise - 2.0 * ahead * ahead
                powers[MID + v] = up
            if MID - v >= 0:
                fall = fall + 2.0 * ahead * ahead
                down = down - fall
                powers[MID - v] = down
        order = [(v + 2) % (SPAN // 8) for v in range(SPAN // 8)]
        g = jnp.exp2(jnp.concatenate([powers[v] for v in order], axis=0)).astype(jnp.bfloat16)
        hit = code_s[s, pl.ds(i, 1), :] == row24
        w = [jnp.where(hit, w_s[a, s, pl.ds(i, 1), :], 0.0) for a in range(3)]
        return g, jnp.concatenate(w, axis=0).astype(jnp.bfloat16)

    def couple(i, at, n):
        both = []
        for k in range(2):
            parts = [factors(i + 8 * k, s) for s in range(n)]
            g = jnp.concatenate([f[0] for f in parts], axis=1)
            w = jnp.concatenate([f[1] for f in parts], axis=1)
            both.append(lax.dot_general(w, g, (((1,), (1,)), ((), ())), preferred_element_type=jnp.float32))
        res_s[pl.ds(pl.multiple_of(at * 72, 8), 72), :] = jnp.concatenate(both, axis=1)

    for n in range(1, slots + 1):
        @pl.when(live == n)
        def _(n=n):
            def body(g, carry):
                for q in range(8 * groups):
                    couple((g * groups + q // 8) * 16 + q % 8, (g * groups + q // 8) * 8 + q % 8, n)
                return carry
            lax.fori_loop(0, beads // (16 * groups), body, 0)

    @pl.when(live == 0)
    def _():
        res_s[...] = jnp.zeros_like(res_s)

    cut = lane % 64

    def unfold(g, carry):
        i0 = g * 16
        kt16 = jnp.broadcast_to(col_s[pl.ds(pl.multiple_of(i0, 16), 16), 3:4], (16, 128))
        is_t = [kt16 == float(t) for t in range(3)]
        for a in range(3):
            d = []
            for t in range(3):
                r = [res_s[pl.ds(g * 8 * 72 + a * 24 + t * 8 + m, 8, stride=72), :] for m in range(8)]
                r = [jnp.zeros_like(lane, jnp.float32)] + r + [jnp.zeros_like(lane, jnp.float32)]
                halves = []
                for v in range(2):
                    m = 4 * v + 1
                    el = jnp.where(cut < 48, r[m], r[m + 2])
                    eu = jnp.where(cut < 48, r[m + 2], r[min(m + 4, 9)])
                    ol = jnp.where(cut < 48, r[m + 1], r[m + 3])
                    ou = jnp.where(cut < 32, r[m + 3], jnp.where(cut < 48, r[m - 1], r[m + 1]))
                    et = pltpu.roll(jnp.where(low, eu, el), 64, 1)
                    ot = pltpu.roll(jnp.where(low, ou, ol), 64, 1)
                    near = jnp.where(low, el, et) + pltpu.roll(jnp.where(low, ol, ot), 32, 1)
                    far = jnp.where(low, et, eu) + pltpu.roll(jnp.where(low, ot, ou), 32, 1)
                    halves.append(jnp.concatenate([near, far], axis=0))
                d.append(halves)
            for p, (lo_t, hi_t) in enumerate(CLASSES):
                for v in range(2):
                    x = jnp.where(is_t[lo_t], d[hi_t][v], 0.0)
                    if lo_t != hi_t:
                        x = jnp.where(is_t[hi_t], d[lo_t][v], x)
                    rows_s[pl.ds(pl.multiple_of((b * 3 + a) * beads + i0, 16), 16), p * K + v * 128:p * K + (v + 1) * 128] = x.astype(jnp.bfloat16)
        return carry
    lax.fori_loop(0, beads // 16, unfold, 0)

    @pl.when(b == pl.num_programs(0) - 1)
    def _():
        gram_tiles(me_ref, force_ref, rows_s, left_s, outs, plan)


def design(off, mask, me, strip, below, above, force, plan, groups=2):
    nb, slots = off.shape
    x_rows, by_blocks, _, beads = strip.shape
    total = nb * 3 * beads
    share = (2, plan.pairs, plan.size_x, plan.slots, plan.part, HALF)
    return pl.pallas_call(
        functools.partial(design_kernel, plan=plan, by_blocks=by_blocks, beads=beads, slots=slots, groups=groups),
        grid_spec=pltpu.PrefetchScalarGridSpec(
            num_scalar_prefetch=3,
            grid=(nb,),
            in_specs=[pl.BlockSpec(strip.shape, lambda b, *_: (0, 0, 0, 0))] * 3
            + [pl.BlockSpec((16, total), lambda b, *_: (0, 0))],
            out_specs=[pl.BlockSpec(share, lambda b, *_: (0,) * 6)] * CHUNKS,
            scratch_shapes=[
                pltpu.VMEM((slots, beads, beads), jnp.float32),
                pltpu.VMEM((slots, beads, beads), jnp.float32),
                pltpu.VMEM((slots, beads, beads), jnp.float32),
                pltpu.VMEM((3, slots, beads, beads), jnp.float32),
                pltpu.VMEM((beads // 2 * 72, 128), jnp.float32),
                pltpu.VMEM((total, PAIRS * K), jnp.bfloat16),
                pltpu.VMEM((K, total), jnp.bfloat16),
                pltpu.VMEM((x_rows * (by_blocks + 2), 8, beads), jnp.float32),
                pltpu.VMEM((beads, 8), jnp.float32),
                pltpu.SMEM((slots + 1,), jnp.int32),
            ],
        ),
        out_shape=[jax.ShapeDtypeStruct(share, jnp.float32)] * CHUNKS,
        compiler_params=pltpu.CompilerParams(vmem_limit_bytes=56 * 1024 * 1024),
    )(off, mask, me, strip, below, above, force)


def pack_kernel(me_ref, send_ref, parts_ref, own_ref, *msg_refs, plan, scale):
    def fetch(ref, j, s):
        for z in range(plan.size_x):
            value = parts_ref[s // plan.slots, z ^ me_ref[2], s % plan.slots]
            ref[j, z * plan.part:(z + 1) * plan.part, :] = value * scale

    for s in range(plan.room):
        fetch(own_ref, s, s)
    at = 0
    for ref, count in zip(msg_refs, plan.counts):
        for j in range(count):
            fetch(ref, j, send_ref[me_ref[1], at + j])
        at += count


def pack(me, parts, plan, scale):
    shapes = [(n, HALF // 2, HALF) for n in [plan.room] + plan.counts]
    return pl.pallas_call(
        functools.partial(pack_kernel, plan=plan, scale=scale),
        grid_spec=pltpu.PrefetchScalarGridSpec(
            num_scalar_prefetch=2,
            grid=(1,),
            in_specs=[pl.BlockSpec(parts.shape, lambda b, *_: (0,) * parts.ndim)],
            out_specs=[pl.BlockSpec(s, lambda b, *_: (0, 0, 0)) for s in shapes],
        ),
        out_shape=[jax.ShapeDtypeStruct(s, jnp.float32) for s in shapes],
        compiler_params=pltpu.CompilerParams(vmem_limit_bytes=32 * 1024 * 1024),
    )(me, jnp.asarray(plan.send), parts)


def place_kernel(me_ref, table_ref, rhs_at_ref, mine_ref, other_ref, gram_ref, rhs_ref, full_s, *, plan):
    half = HALF // 2
    core = me_ref[0]
    dev = me_ref[3]
    full_s[:, pl.ds(pl.multiple_of(core * half, half), half), :] = mine_ref[...]
    full_s[:, pl.ds(pl.multiple_of((1 - core) * half, half), half), :] = other_ref[...]
    for u in range(plan.rows // plan.unit):
        at = (dev * plan.rows + u * plan.unit) % HALF
        for c in range(TILES):
            entry = table_ref[dev, u * TILES + c]
            cut = (slice(u * plan.unit, (u + 1) * plan.unit), slice(c * HALF, (c + 1) * HALF))

            @pl.when(entry < 0)
            def _(cut=cut):
                gram_ref[cut] = jnp.zeros((plan.unit, HALF), jnp.float32)

            @pl.when(jnp.logical_and(entry >= 0, entry % 2 == 0))
            def _(cut=cut, entry=entry, at=at):
                gram_ref[cut] = full_s[entry // 2, pl.ds(pl.multiple_of(at, plan.unit), plan.unit), :]

            @pl.when(jnp.logical_and(entry >= 0, entry % 2 == 1))
            def _(cut=cut, entry=entry, at=at):
                turned = full_s[entry // 2].T
                value = turned[0:plan.unit]
                for v in range(1, HALF // plan.unit):
                    value = jnp.where(at == v * plan.unit, turned[v * plan.unit:(v + 1) * plan.unit], value)
                gram_ref[cut] = value
    for u in range(plan.rows // plan.unit):
        at = dev * plan.rows + u * plan.unit
        line = full_s[rhs_at_ref[dev], pl.ds(at // HALF, 1), :]
        value = line[:, 0:plan.unit]
        for v in range(1, HALF // plan.unit):
            value = jnp.where(at % HALF == v * plan.unit, line[:, v * plan.unit:(v + 1) * plan.unit], value)
        rhs_ref[:, u * plan.unit:(u + 1) * plan.unit] = value


def place(me, mine, other, plan):
    return pl.pallas_call(
        functools.partial(place_kernel, plan=plan),
        grid_spec=pltpu.PrefetchScalarGridSpec(
            num_scalar_prefetch=3,
            grid=(1,),
            in_specs=[pl.BlockSpec(mine.shape, lambda b, *_: (0, 0, 0))] * 2,
            out_specs=[
                pl.BlockSpec((plan.rows, PAIRS * K), lambda b, *_: (0, 0)),
                pl.BlockSpec((1, plan.rows), lambda b, *_: (0, 0)),
            ],
            scratch_shapes=[pltpu.VMEM((plan.entries, HALF, HALF), jnp.float32)],
        ),
        out_shape=[
            jax.ShapeDtypeStruct((plan.rows, PAIRS * K), jnp.float32),
            jax.ShapeDtypeStruct((1, plan.rows), jnp.float32),
        ],
        compiler_params=pltpu.CompilerParams(vmem_limit_bytes=32 * 1024 * 1024),
    )(me, jnp.asarray(plan.table), jnp.asarray(plan.rhs), mine, other)


def shifted(x, axis, step):
    count = lax.axis_size(axis)
    return lax.ppermute(x, axis, [(i, (i + step) % count) for i in range(count)])


def swap(x, axis, flip):
    return lax.ppermute(x, axis, [(i, i ^ flip) for i in range(lax.axis_size(axis))])


def summed(x, plan):
    x = x[0] + swap(x[1], "gy", 1)
    got = [swap(x[k], "gy", 2 * k) for k in range(1, plan.pairs)]
    x = functools.reduce(jnp.add, got, x[0])
    got = [swap(x[k], "gx", k) for k in range(1, plan.size_x)]
    x = functools.reduce(jnp.add, got, x[0])
    return jnp.stack([x] + [swap(x, "gx", k) for k in range(1, plan.size_x)])


def shards(coords, kinds, forces, tile_offsets, tile_mask):
    frames, _, blocks_x, blocks_y, beads = coords.shape
    slots = tile_offsets.shape[3]
    nb = blocks_x * blocks_y
    size_x, size_y = lax.axis_size("gx"), lax.axis_size("gy")
    frame_rows = 3 * beads * nb * size_x * size_y
    plan = Plan(size_x, size_y)
    dev = lax.axis_index("gy")
    me = jnp.stack([dev % 2, dev // 2, lax.axis_index("gx"), dev]).astype(jnp.int32)
    cells = jnp.concatenate(
        [jnp.transpose(coords[0], (1, 2, 0, 3)), kinds.astype(jnp.float32)[:, :, None, :]], axis=2
    )
    left, right = shifted(cells, "gx", 1), shifted(cells, "gx", -1)
    strip = jnp.concatenate([left[-1:], cells, right[:1]], axis=0)
    below, above = shifted(strip, "gy", 1), shifted(strip, "gy", -1)
    force = jnp.transpose(forces[0], (1, 2, 0, 3)).reshape(1, nb * 3 * beads)
    chunks = design(
        tile_offsets.reshape(nb, slots),
        tile_mask.reshape(nb, slots),
        me,
        strip,
        below,
        above,
        jnp.broadcast_to(force, (16, nb * 3 * beads)),
        plan,
    )
    parts = jnp.stack([summed(x, plan) for x in chunks])
    own, *messages = pack(me, parts, plan, 1.0 / frame_rows)
    got = [swap(m, "gy", 2 * k) for k, m in enumerate(messages, 1)]
    mine = jnp.concatenate([own] + got)
    gram, rhs = place(me, mine, swap(mine, "gy", 1), plan)
    return gram[None], rhs


def solution(mesh):
    placed = (
        P(None, None, "gx", "gy", None),
        P("gx", "gy", None),
        P(None, None, "gx", "gy", None),
        P(None, "gx", "gy", None),
        P(None, "gx", "gy", None),
    )
    return jax.shard_map(
        shards,
        mesh=mesh,
        in_specs=placed,
        out_specs=(P(None, "gy", None), P(None, "gy")),
        check_vma=False,
    )
```

```python
import functools
import math
import jax
import jax.numpy as jnp
import numpy as np
from jax import lax
from jax.experimental import pallas as pl
from jax.experimental.pallas import tpu as pltpu
from jax.sharding import PartitionSpec as P

K=256; PAIRS=6
STEP=32; SPAN=64
ROOT=math.sqrt(0.5*math.log2(math.e))
NEG=-1e9
MID=3

CLASSES = ((0, 0), (0, 1), (0, 2), (1, 1), (1, 2), (2, 2))
HALF = 128
TILES = PAIRS * K // HALF
CHUNKS = 2
RHS = (-1, -1)


def stored(r, c):
    p, q = CLASSES[r * HALF // K], CLASSES[c * HALF // K]
    return r <= c and bool(set(p) & set(q))


class Plan:
    def __init__(self, size_x, size_y):
        self.size_x = size_x
        self.pairs = size_y // 2
        self.rows = PAIRS * K // size_y
        self.part = HALF // 2 // size_x
        pairs = range(self.pairs)
        tiles = [(r, c) for r in range(TILES) for c in range(TILES) if stored(r, c)]
        needs = {RHS: set(pairs)}
        for r, c in tiles:
            span = [(x * HALF, x * HALF + HALF) for x in (r, c)]
            needs[(r, c)] = {
                g for g in pairs for lo, hi in span
                if lo < (g + 1) * 2 * self.rows and hi > g * 2 * self.rows
            }
        self.slots = -(-(len(tiles) + 1) // (self.pairs * CHUNKS))
        room = self.slots * CHUNKS
        owned = [[] for _ in pairs]
        for tile in sorted(tiles, key=lambda t: len(needs[t])) + [RHS]:
            free = [g for g in pairs if len(owned[g]) < room]
            wanted = [g for g in free if g in needs[tile]] or free
            owned[min(wanted, key=lambda g: len(owned[g]))].append(tile)
        self.owned = owned
        self.place = {t: (g, s) for g in pairs for s, t in enumerate(owned[g])}
        lists = {
            (g, k): [s for s, t in enumerate(owned[g]) if (g ^ k) in needs[t]]
            for g in pairs for k in range(1, self.pairs)
        }
        self.counts = [max(1, max(len(lists[g, k]) for g in pairs)) for k in range(1, self.pairs)]
        self.room = room
        self.send = np.zeros((self.pairs, sum(self.counts)), np.int32)
        self.entries = room + sum(self.counts)
        found = []
        for g in pairs:
            where = {t: s for s, t in enumerate(owned[g])}
            at = 0
            for k in range(1, self.pairs):
                chosen = lists[g, k]
                self.send[g, at:at + len(chosen)] = chosen
                for j, s in enumerate(lists[g ^ k, k]):
                    where[owned[g ^ k][s]] = room + at + j
                at += self.counts[k - 1]
            found.append(where)
        self.unit = math.gcd(self.rows, HALF)
        units = self.rows // self.unit
        self.table = np.zeros((size_y, units * TILES), np.int32)
        self.rhs = np.zeros((size_y,), np.int32)
        for d in range(size_y):
            where = found[d // 2]
            self.rhs[d] = where[RHS]
            for u in range(units):
                r = (d * self.rows + u * self.unit) // HALF
                for c in range(TILES):
                    if stored(r, c):
                        self.table[d, u * TILES + c] = 2 * where[(r, c)]
                    elif stored(c, r):
                        self.table[d, u * TILES + c] = 2 * where[(c, r)] + 1
                    else:
                        self.table[d, u * TILES + c] = -1


def gram_tiles(me_ref, force_ref, rows_s, left_s, upper, lower, plan):
    def put(tile, value):
        g, s = plan.place[tile]
        for h in range(2):
            for z in range(plan.size_x):
                at = h * HALF // 2 + z * plan.part
                out = (upper, lower)[h][s // plan.slots]
                out[g ^ me_ref[1], z ^ me_ref[2], s % plan.slots] = value[at:at + plan.part]

    used = {(g, s) for g, s in plan.place.values()}
    for g in range(plan.pairs):
        for s in range(plan.room):
            if (g, s) not in used:
                for out in (upper, lower):
                    for z in range(plan.size_x):
                        out[s // plan.slots][g ^ me_ref[1], z ^ me_ref[2], s % plan.slots] = jnp.zeros((plan.part, HALF), jnp.float32)
    for p in range(PAIRS):
        left_s[...] = rows_s[:, p * K:(p + 1) * K].T
        for q in range(p, PAIRS):
            if not stored(2 * p, 2 * q):
                continue
            block = jnp.dot(left_s[...], rows_s[:, q * K:(q + 1) * K], preferred_element_type=jnp.float32)
            for r in range(2):
                for c in range(2):
                    if stored(2 * p + r, 2 * q + c):
                        put((2 * p + r, 2 * q + c), block[r * HALF:(r + 1) * HALF, c * HALF:(c + 1) * HALF])
    rhs = jnp.dot(force_ref[...], rows_s[...], preferred_element_type=jnp.float32)
    lines = [rhs[0:1, t * HALF:(t + 1) * HALF] for t in range(TILES)]
    put(RHS, jnp.concatenate(lines + [jnp.zeros((HALF - TILES, HALF), jnp.float32)], axis=0))


def design_kernel(off_ref, mask_ref, me_ref, strip_ref, below_ref, above_ref, force_ref, *refs, plan, by_blocks, beads, slots, groups):
    outs = refs[:2 * CHUNKS]
    pos_s, lt_s, code_s, w_s, res_s, rows_s, left_s, near_s, col_s, list_s = refs[2 * CHUNKS:]
    b = pl.program_id(0)
    bx = b // by_blocks
    by = b % by_blocks
    live = jnp.int32(0)
    for t in range(slots):
        list_s[live] = off_ref[b, t]
        live = live + mask_ref[b, t]

    @pl.when(b == 0)
    def _():
        near_s[...] = jnp.zeros_like(near_s)
        for x in range(strip_ref.shape[0]):
            near_s[x * (by_blocks + 2), 0:4] = below_ref[x, by_blocks - 1]
            for y in range(by_blocks):
                near_s[x * (by_blocks + 2) + y + 1, 0:4] = strip_ref[x, y]
            near_s[x * (by_blocks + 2) + by_blocks + 1, 0:4] = above_ref[x, 0]

    col_s[...] = near_s[(bx + 1) * (by_blocks + 2) + by + 1].T
    colv = [jnp.broadcast_to(col_s[:, a:a + 1], (beads, beads)) for a in range(3)]

    def geom(s, c):
        o = list_s[s]
        ox = o // 3
        oy = o % 3
        src = (bx + ox) * (by_blocks + 2) + by + oy
        sx = (ox - 1).astype(jnp.float32)
        sy = (oy - 1).astype(jnp.float32)
        d0 = colv[0] - near_s[src, 0:1, :] - sx
        d1 = colv[1] - near_s[src, 1:2, :] - sy
        d2 = colv[2] - near_s[src, 2:3, :]
        r2 = d0 * d0 + d1 * d1 + d2 * d2
        u = jnp.sqrt(r2) * K
        m = jnp.minimum(jnp.floor(u * (1.0 / STEP)), K // STEP - 1.0)
        pos_s[s] = (u - m * STEP) * ROOT
        t = jnp.maximum(1.0 - r2, 0.0)
        lt_s[s] = jnp.where(t > 0.0, 2.0 * jnp.log2(jnp.where(t > 0.0, t, 1.0)), NEG)
        code_s[s] = near_s[src, 3:4, :] * 8.0 + m
        sc = 1.0 / jnp.sqrt(r2 + 0.05)
        w_s[0, s] = d0 * sc
        w_s[1, s] = d1 * sc
        w_s[2, s] = d2 * sc
        return c
    lax.fori_loop(0, live, geom, 0)
    middle = (lax.broadcasted_iota(jnp.int32, (8, beads), 0).astype(jnp.float32) + (8 * MID - 15.5)) * ROOT
    row24 = lax.broadcasted_iota(jnp.int32, (24, beads), 0).astype(jnp.float32)
    lane = lax.broadcasted_iota(jnp.int32, (8, 128), 1)
    low = lane < 64
    ahead = 8.0 * ROOT

    def factors(i, s):
        x = pos_s[s, pl.ds(i, 1), :] - middle
        up = lt_s[s, pl.ds(i, 1), :] - x * x
        down = up
        rise = x * (2.0 * ahead) - ahead * ahead
        fall = rise
        powers = {MID: up}
        for v in range(1, SPAN // 8):
            if MID + v < SPAN // 8:
                up = up + rise
                rise = rise - 2.0 * ahead * ahead
                powers[MID + v] = up
            if MID - v >= 0:
                fall = fall + 2.0 * ahead * ahead
                down = down - fall
                powers[MID - v] = down
        order = [(v + 2) % (SPAN // 8) for v in range(SPAN // 8)]
        g = jnp.exp2(jnp.concatenate([powers[v] for v in order], axis=0)).astype(jnp.bfloat16)
        hit = code_s[s, pl.ds(i, 1), :] == row24
        w = [jnp.where(hit, w_s[a, s, pl.ds(i, 1), :], 0.0) for a in range(3)]
        return g, jnp.concatenate(w, axis=0).astype(jnp.bfloat16)

    def couple(i, at, n):
        both = []
        for k in range(2):
            parts = [factors(i + 8 * k, s) for s in range(n)]
            g = jnp.concatenate([f[0] for f in parts], axis=1)
            w = jnp.concatenate([f[1] for f in parts], axis=1)
            both.append(lax.dot_general(w, g, (((1,), (1,)), ((), ())), preferred_element_type=jnp.float32))
        res_s[pl.ds(pl.multiple_of(at * 72, 8), 72), :] = jnp.concatenate(both, axis=1)

    cut = lane % 64

    def unfold(g):
        i0 = g * 16
        kt16 = jnp.broadcast_to(col_s[pl.ds(pl.multiple_of(i0, 16), 16), 3:4], (16, 128))
        is_t = [kt16 == float(t) for t in range(3)]
        for a in range(3):
            d = []
            for t in range(3):
                r = [res_s[pl.ds(g * 8 * 72 + a * 24 + t * 8 + m, 8, stride=72), :] for m in range(8)]
                r = [jnp.zeros_like(lane, jnp.float32)] + r + [jnp.zeros_like(lane, jnp.float32)]
                halves = []
                for v in range(2):
                    m = 4 * v + 1
                    el = jnp.where(cut < 48, r[m], r[m + 2])
                    eu = jnp.where(cut < 48, r[m + 2], r[min(m + 4, 9)])
                    ol = jnp.where(cut < 48, r[m + 1], r[m + 3])
                    ou = jnp.where(cut < 32, r[m + 3], jnp.where(cut < 48, r[m - 1], r[m + 1]))
                    et = pltpu.roll(jnp.where(low, eu, el), 64, 1)
                    ot = pltpu.roll(jnp.where(low, ou, ol), 64, 1)
                    near = jnp.where(low, el, et) + pltpu.roll(jnp.where(low, ol, ot), 32, 1)
                    far = jnp.where(low, et, eu) + pltpu.roll(jnp.where(low, ot, ou), 32, 1)
                    halves.append(jnp.concatenate([near, far], axis=0))
                d.append(halves)
            for p, (lo_t, hi_t) in enumerate(CLASSES):
                for v in range(2):
                    x = jnp.where(is_t[lo_t], d[hi_t][v], 0.0)
                    if lo_t != hi_t:
                        x = jnp.where(is_t[hi_t], d[lo_t][v], x)
                    rows_s[pl.ds(pl.multiple_of((b * 3 + a) * beads + i0, 16), 16), p * K + v * 128:p * K + (v + 1) * 128] = x.astype(jnp.bfloat16)
    for n in range(1, slots + 1):
        @pl.when(live == n)
        def _(n=n):
            step = groups if n > slots // 2 else 1

            def body(g, carry):
                for q in range(step):
                    for k in range(8):
                        couple((g * step + q) * 16 + k, (g * step + q) * 8 + k, n)
                    if q > 0:
                        unfold(g * step + q - 1)
                unfold(g * step + step - 1)
                return carry
            lax.fori_loop(0, beads // (16 * step), body, 0)

    @pl.when(live == 0)
    def _():
        rows_s[pl.ds(pl.multiple_of(b * 3 * beads, 16), 3 * beads), :] = jnp.zeros((3 * beads, PAIRS * K), jnp.bfloat16)

    @pl.when(b == pl.num_programs(0) - 1)
    def _():
        for core in range(2):
            @pl.when(me_ref[0] == core)
            def _(core=core):
                gram_tiles(me_ref, force_ref, rows_s, left_s, outs[core::2], outs[1 - core::2], plan)


def design(off, mask, me, strip, below, above, force, plan, groups=4):
    nb, slots = off.shape
    x_rows, by_blocks, _, beads = strip.shape
    total = nb * 3 * beads
    share = (plan.pairs, plan.size_x, plan.slots, plan.part, HALF)
    return pl.pallas_call(
        functools.partial(design_kernel, plan=plan, by_blocks=by_blocks, beads=beads, slots=slots, groups=groups),
        grid_spec=pltpu.PrefetchScalarGridSpec(
            num_scalar_prefetch=3,
            grid=(nb,),
            in_specs=[pl.BlockSpec(strip.shape, lambda b, *_: (0, 0, 0, 0))] * 3
            + [pl.BlockSpec((16, total), lambda b, *_: (0, 0))],
            out_specs=[pl.BlockSpec(share, lambda b, *_: (0,) * 5)] * (2 * CHUNKS),
            scratch_shapes=[
                pltpu.VMEM((slots, beads, beads), jnp.float32),
                pltpu.VMEM((slots, beads, beads), jnp.float32),
                pltpu.VMEM((slots, beads, beads), jnp.float32),
                pltpu.VMEM((3, slots, beads, beads), jnp.float32),
                pltpu.VMEM((beads // 2 * 72, 128), jnp.float32),
                pltpu.VMEM((total, PAIRS * K), jnp.bfloat16),
                pltpu.VMEM((K, total), jnp.bfloat16),
                pltpu.VMEM((x_rows * (by_blocks + 2), 8, beads), jnp.float32),
                pltpu.VMEM((beads, 8), jnp.float32),
                pltpu.SMEM((slots + 1,), jnp.int32),
            ],
        ),
        out_shape=[jax.ShapeDtypeStruct(share, jnp.float32)] * (2 * CHUNKS),
        compiler_params=pltpu.CompilerParams(vmem_limit_bytes=56 * 1024 * 1024),
    )(off, mask, me, strip, below, above, force)


def pack_kernel(me_ref, send_ref, parts_ref, own_ref, *msg_refs, plan, scale):
    def fetch(ref, j, s):
        for z in range(plan.size_x):
            value = parts_ref[s // plan.slots, z ^ me_ref[2], s % plan.slots]
            ref[j, z * plan.part:(z + 1) * plan.part, :] = value * scale

    for s in range(plan.room):
        fetch(own_ref, s, s)
    at = 0
    for ref, count in zip(msg_refs, plan.counts):
        for j in range(count):
            fetch(ref, j, send_ref[me_ref[1], at + j])
        at += count


def pack(me, parts, plan, scale):
    shapes = [(n, HALF // 2, HALF) for n in [plan.room] + plan.counts]
    return pl.pallas_call(
        functools.partial(pack_kernel, plan=plan, scale=scale),
        grid_spec=pltpu.PrefetchScalarGridSpec(
            num_scalar_prefetch=2,
            grid=(1,),
            in_specs=[pl.BlockSpec(parts.shape, lambda b, *_: (0,) * parts.ndim)],
            out_specs=[pl.BlockSpec(s, lambda b, *_: (0, 0, 0)) for s in shapes],
        ),
        out_shape=[jax.ShapeDtypeStruct(s, jnp.float32) for s in shapes],
        compiler_params=pltpu.CompilerParams(vmem_limit_bytes=32 * 1024 * 1024),
    )(me, jnp.asarray(plan.send), parts)


def place_kernel(me_ref, table_ref, rhs_at_ref, mine_ref, other_ref, gram_ref, rhs_ref, full_s, *, plan):
    half = HALF // 2
    core = me_ref[0]
    dev = me_ref[3]
    full_s[:, pl.ds(pl.multiple_of(core * half, half), half), :] = mine_ref[...]
    full_s[:, pl.ds(pl.multiple_of((1 - core) * half, half), half), :] = other_ref[...]
    for u in range(plan.rows // plan.unit):
        at = (dev * plan.rows + u * plan.unit) % HALF
        for c in range(TILES):
            entry = table_ref[dev, u * TILES + c]
            cut = (slice(u * plan.unit, (u + 1) * plan.unit), slice(c * HALF, (c + 1) * HALF))

            @pl.when(entry < 0)
            def _(cut=cut):
                gram_ref[cut] = jnp.zeros((plan.unit, HALF), jnp.float32)

            @pl.when(jnp.logical_and(entry >= 0, entry % 2 == 0))
            def _(cut=cut, entry=entry, at=at):
                gram_ref[cut] = full_s[entry // 2, pl.ds(pl.multiple_of(at, plan.unit), plan.unit), :]

            @pl.when(jnp.logical_and(entry >= 0, entry % 2 == 1))
            def _(cut=cut, entry=entry, at=at):
                turned = full_s[entry // 2].T
                value = turned[0:plan.unit]
                for v in range(1, HALF // plan.unit):
                    value = jnp.where(at == v * plan.unit, turned[v * plan.unit:(v + 1) * plan.unit], value)
                gram_ref[cut] = value
    for u in range(plan.rows // plan.unit):
        at = dev * plan.rows + u * plan.unit
        line = full_s[rhs_at_ref[dev], pl.ds(at // HALF, 1), :]
        value = line[:, 0:plan.unit]
        for v in range(1, HALF // plan.unit):
            value = jnp.where(at % HALF == v * plan.unit, line[:, v * plan.unit:(v + 1) * plan.unit], value)
        rhs_ref[:, u * plan.unit:(u + 1) * plan.unit] = value


def place(me, mine, other, plan):
    return pl.pallas_call(
        functools.partial(place_kernel, plan=plan),
        grid_spec=pltpu.PrefetchScalarGridSpec(
            num_scalar_prefetch=3,
            grid=(1,),
            in_specs=[pl.BlockSpec(mine.shape, lambda b, *_: (0, 0, 0))] * 2,
            out_specs=[
                pl.BlockSpec((plan.rows, PAIRS * K), lambda b, *_: (0, 0)),
                pl.BlockSpec((1, plan.rows), lambda b, *_: (0, 0)),
            ],
            scratch_shapes=[pltpu.VMEM((plan.entries, HALF, HALF), jnp.float32)],
        ),
        out_shape=[
            jax.ShapeDtypeStruct((plan.rows, PAIRS * K), jnp.float32),
            jax.ShapeDtypeStruct((1, plan.rows), jnp.float32),
        ],
        compiler_params=pltpu.CompilerParams(vmem_limit_bytes=32 * 1024 * 1024),
    )(me, jnp.asarray(plan.table), jnp.asarray(plan.rhs), mine, other)


def shifted(x, axis, step):
    count = lax.axis_size(axis)
    return lax.ppermute(x, axis, [(i, (i + step) % count) for i in range(count)])


def swap(x, axis, flip):
    return lax.ppermute(x, axis, [(i, i ^ flip) for i in range(lax.axis_size(axis))])


def summed(x, away, plan):
    x = x + swap(away, "gy", 1)
    got = [swap(x[k], "gy", 2 * k) for k in range(1, plan.pairs)]
    x = functools.reduce(jnp.add, got, x[0])
    got = [swap(x[k], "gx", k) for k in range(1, plan.size_x)]
    x = functools.reduce(jnp.add, got, x[0])
    return jnp.stack([x] + [swap(x, "gx", k) for k in range(1, plan.size_x)])


def shards(coords, kinds, forces, tile_offsets, tile_mask):
    frames, _, blocks_x, blocks_y, beads = coords.shape
    slots = tile_offsets.shape[3]
    nb = blocks_x * blocks_y
    size_x, size_y = lax.axis_size("gx"), lax.axis_size("gy")
    frame_rows = 3 * beads * nb * size_x * size_y
    plan = Plan(size_x, size_y)
    dev = lax.axis_index("gy")
    me = jnp.stack([dev % 2, dev // 2, lax.axis_index("gx"), dev]).astype(jnp.int32)
    cells = jnp.concatenate(
        [jnp.transpose(coords[0], (1, 2, 0, 3)), kinds.astype(jnp.float32)[:, :, None, :]], axis=2
    )
    left, right = shifted(cells, "gx", 1), shifted(cells, "gx", -1)
    strip = jnp.concatenate([left[-1:], cells, right[:1]], axis=0)
    below, above = shifted(strip, "gy", 1), shifted(strip, "gy", -1)
    force = jnp.transpose(forces[0], (1, 2, 0, 3)).reshape(1, nb * 3 * beads)
    chunks = design(
        tile_offsets.reshape(nb, slots),
        tile_mask.reshape(nb, slots),
        me,
        strip,
        below,
        above,
        jnp.broadcast_to(force, (16, nb * 3 * beads)),
        plan,
    )
    parts = jnp.stack([summed(*chunks[2 * c:2 * c + 2], plan) for c in range(CHUNKS)])
    own, *messages = pack(me, parts, plan, 1.0 / frame_rows)
    got = [swap(m, "gy", 2 * k) for k, m in enumerate(messages, 1)]
    mine = jnp.concatenate([own] + got)
    gram, rhs = place(me, mine, swap(mine, "gy", 1), plan)
    return gram[None], rhs


def solution(mesh):
    placed = (
        P(None, None, "gx", "gy", None),
        P("gx", "gy", None),
        P(None, None, "gx", "gy", None),
        P(None, "gx", "gy", None),
        P(None, "gx", "gy", None),
    )
    return jax.shard_map(
        shards,
        mesh=mesh,
        in_specs=placed,
        out_specs=(P(None, "gy", None), P(None, "gy")),
        check_vma=False,
    )
```

```python
import functools
import math
import jax
import jax.numpy as jnp
import numpy as np
from jax import lax
from jax.experimental import pallas as pl
from jax.experimental.pallas import tpu as pltpu
from jax.sharding import PartitionSpec as P

K=256; PAIRS=6
STEP=32; SPAN=64
ROOT=math.sqrt(0.5*math.log2(math.e))
NEG=-1e9
MID=3

CLASSES = ((0, 0), (0, 1), (0, 2), (1, 1), (1, 2), (2, 2))
HALF = 128
TILES = PAIRS * K // HALF
CHUNKS = 2
RHS = (-1, -1)


def stored(r, c):
    p, q = CLASSES[r * HALF // K], CLASSES[c * HALF // K]
    return r <= c and bool(set(p) & set(q))


class Plan:
    def __init__(self, size_x, size_y):
        self.size_x = size_x
        self.pairs = size_y // 2
        self.rows = PAIRS * K // size_y
        self.part = HALF // 2 // size_x
        pairs = range(self.pairs)
        tiles = [(r, c) for r in range(TILES) for c in range(TILES) if stored(r, c)]
        needs = {RHS: set(pairs)}
        for r, c in tiles:
            span = [(x * HALF, x * HALF + HALF) for x in (r, c)]
            needs[(r, c)] = {
                g for g in pairs for lo, hi in span
                if lo < (g + 1) * 2 * self.rows and hi > g * 2 * self.rows
            }
        self.slots = -(-(len(tiles) + 1) // (self.pairs * CHUNKS))
        room = self.slots * CHUNKS
        owned = [[] for _ in pairs]
        for tile in sorted(tiles, key=lambda t: len(needs[t])) + [RHS]:
            free = [g for g in pairs if len(owned[g]) < room]
            wanted = [g for g in free if g in needs[tile]] or free
            owned[min(wanted, key=lambda g: len(owned[g]))].append(tile)
        self.owned = owned
        self.place = {t: (g, s) for g in pairs for s, t in enumerate(owned[g])}
        lists = {
            (g, k): [s for s, t in enumerate(owned[g]) if (g ^ k) in needs[t]]
            for g in pairs for k in range(1, self.pairs)
        }
        self.counts = [max(1, max(len(lists[g, k]) for g in pairs)) for k in range(1, self.pairs)]
        self.room = room
        self.send = np.zeros((self.pairs, sum(self.counts)), np.int32)
        self.entries = room + sum(self.counts)
        found = []
        for g in pairs:
            where = {t: s for s, t in enumerate(owned[g])}
            at = 0
            for k in range(1, self.pairs):
                chosen = lists[g, k]
                self.send[g, at:at + len(chosen)] = chosen
                for j, s in enumerate(lists[g ^ k, k]):
                    where[owned[g ^ k][s]] = room + at + j
                at += self.counts[k - 1]
            found.append(where)
        self.unit = math.gcd(self.rows, HALF)
        units = self.rows // self.unit
        self.table = np.zeros((size_y, units * TILES), np.int32)
        self.rhs = np.zeros((size_y,), np.int32)
        for d in range(size_y):
            where = found[d // 2]
            self.rhs[d] = where[RHS]
            for u in range(units):
                r = (d * self.rows + u * self.unit) // HALF
                for c in range(TILES):
                    if stored(r, c):
                        self.table[d, u * TILES + c] = 2 * where[(r, c)]
                    elif stored(c, r):
                        self.table[d, u * TILES + c] = 2 * where[(c, r)] + 1
                    else:
                        self.table[d, u * TILES + c] = -1


def gram_tiles(me_ref, force_ref, rows_s, left_s, outs, plan):
    def put(tile, value):
        g, s = plan.place[tile]
        out = outs[s // plan.slots]
        for h in range(2):
            for z in range(plan.size_x):
                at = h * HALF // 2 + z * plan.part
                out[h ^ me_ref[0], g ^ me_ref[1], z ^ me_ref[2], s % plan.slots] = value[at:at + plan.part]

    used = {(g, s) for g, s in plan.place.values()}
    for g in range(plan.pairs):
        for s in range(plan.room):
            if (g, s) not in used:
                plan_tile = jnp.zeros((plan.part, HALF), jnp.float32)
                for h in range(2):
                    for z in range(plan.size_x):
                        outs[s // plan.slots][h ^ me_ref[0], g ^ me_ref[1], z ^ me_ref[2], s % plan.slots] = plan_tile
    for p in range(PAIRS):
        left_s[...] = rows_s[:, p * K:(p + 1) * K].T
        for q in range(p, PAIRS):
            if not stored(2 * p, 2 * q):
                continue
            block = jnp.dot(left_s[...], rows_s[:, q * K:(q + 1) * K], preferred_element_type=jnp.float32)
            for r in range(2):
                for c in range(2):
                    if stored(2 * p + r, 2 * q + c):
                        put((2 * p + r, 2 * q + c), block[r * HALF:(r + 1) * HALF, c * HALF:(c + 1) * HALF])
    rhs = jnp.dot(force_ref[...], rows_s[...], preferred_element_type=jnp.float32)
    lines = [rhs[0:1, t * HALF:(t + 1) * HALF] for t in range(TILES)]
    put(RHS, jnp.concatenate(lines + [jnp.zeros((HALF - TILES, HALF), jnp.float32)], axis=0))


def design_kernel(off_ref, mask_ref, me_ref, strip_ref, below_ref, above_ref, force_ref, *refs, plan, by_blocks, beads, slots, groups):
    outs = refs[:CHUNKS]
    pos_s, lt_s, code_s, w_s, res_s, rows_s, left_s, near_s, col_s, list_s = refs[CHUNKS:]
    b = pl.program_id(0)
    bx = b // by_blocks
    by = b % by_blocks
    live = jnp.int32(0)
    for t in range(slots):
        list_s[live] = off_ref[b, t]
        live = live + mask_ref[b, t]

    @pl.when(b == 0)
    def _():
        near_s[...] = jnp.zeros_like(near_s)
        for x in range(strip_ref.shape[0]):
            near_s[x * (by_blocks + 2), 0:4] = below_ref[x, by_blocks - 1]
            for y in range(by_blocks):
                near_s[x * (by_blocks + 2) + y + 1, 0:4] = strip_ref[x, y]
            near_s[x * (by_blocks + 2) + by_blocks + 1, 0:4] = above_ref[x, 0]

    col_s[...] = near_s[(bx + 1) * (by_blocks + 2) + by + 1].T
    colv = [jnp.broadcast_to(col_s[:, a:a + 1], (beads, beads)) for a in range(3)]

    def geom(s, c):
        o = list_s[s]
        ox = o // 3
        oy = o % 3
        src = (bx + ox) * (by_blocks + 2) + by + oy
        sx = (ox - 1).astype(jnp.float32)
        sy = (oy - 1).astype(jnp.float32)
        d0 = colv[0] - near_s[src, 0:1, :] - sx
        d1 = colv[1] - near_s[src, 1:2, :] - sy
        d2 = colv[2] - near_s[src, 2:3, :]
        r2 = d0 * d0 + d1 * d1 + d2 * d2
        u = jnp.sqrt(r2) * K
        m = jnp.minimum(jnp.floor(u * (1.0 / STEP)), K // STEP - 1.0)
        pos_s[s] = (u - m * STEP) * ROOT
        t = jnp.maximum(1.0 - r2, 0.0)
        lt_s[s] = jnp.where(t > 0.0, 2.0 * jnp.log2(jnp.where(t > 0.0, t, 1.0)), NEG)
        code_s[s] = near_s[src, 3:4, :] * 8.0 + m
        sc = 1.0 / jnp.sqrt(r2 + 0.05)
        w_s[0, s] = d0 * sc
        w_s[1, s] = d1 * sc
        w_s[2, s] = d2 * sc
        return c
    lax.fori_loop(0, live, geom, 0)
    middle = (lax.broadcasted_iota(jnp.int32, (8, beads), 0).astype(jnp.float32) + (8 * MID - 15.5)) * ROOT
    row24 = lax.broadcasted_iota(jnp.int32, (24, beads), 0).astype(jnp.float32)
    lane = lax.broadcasted_iota(jnp.int32, (8, 128), 1)
    low = lane < 64
    ahead = 8.0 * ROOT

    def factors(i, s):
        x = pos_s[s, pl.ds(i, 1), :] - middle
        up = lt_s[s, pl.ds(i, 1), :] - x * x
        down = up
        rise = x * (2.0 * ahead) - ahead * ahead
        fall = rise
        powers = {MID: up}
        for v in range(1, SPAN // 8):
            if MID + v < SPAN // 8:
                up = up + rise
                rise = rise - 2.0 * ahead * ahead
                powers[MID + v] = up
            if MID - v >= 0:
                fall = fall + 2.0 * ahead * ahead
                down = down - fall
                powers[MID - v] = down
        order = [(v + 2) % (SPAN // 8) for v in range(SPAN // 8)]
        g = jnp.exp2(jnp.concatenate([powers[v] for v in order], axis=0)).astype(jnp.bfloat16)
        hit = code_s[s, pl.ds(i, 1), :] == row24
        w = [jnp.where(hit, w_s[a, s, pl.ds(i, 1), :], 0.0) for a in range(3)]
        return g, jnp.concatenate(w, axis=0).astype(jnp.bfloat16)

    def couple(i, at, n):
        both = []
        for k in range(2):
            parts = [factors(i + 8 * k, s) for s in range(n)]
            g = jnp.concatenate([f[0] for f in parts], axis=1)
            w = jnp.concatenate([f[1] for f in parts], axis=1)
            both.append(lax.dot_general(w, g, (((1,), (1,)), ((), ())), preferred_element_type=jnp.float32))
        res_s[pl.ds(pl.multiple_of(at * 72, 8), 72), :] = jnp.concatenate(both, axis=1)

    cut = lane % 64

    def unfold(g):
        i0 = g * 16
        kt16 = jnp.broadcast_to(col_s[pl.ds(pl.multiple_of(i0, 16), 16), 3:4], (16, 128))
        is_t = [kt16 == float(t) for t in range(3)]
        for a in range(3):
            d = []
            for t in range(3):
                r = [res_s[pl.ds(g * 8 * 72 + a * 24 + t * 8 + m, 8, stride=72), :] for m in range(8)]
                r = [jnp.zeros_like(lane, jnp.float32)] + r + [jnp.zeros_like(lane, jnp.float32)]
                halves = []
                for v in range(2):
                    m = 4 * v + 1
                    el = jnp.where(cut < 48, r[m], r[m + 2])
                    eu = jnp.where(cut < 48, r[m + 2], r[min(m + 4, 9)])
                    ol = jnp.where(cut < 48, r[m + 1], r[m + 3])
                    ou = jnp.where(cut < 32, r[m + 3], jnp.where(cut < 48, r[m - 1], r[m + 1]))
                    et = pltpu.roll(jnp.where(low, eu, el), 64, 1)
                    ot = pltpu.roll(jnp.where(low, ou, ol), 64, 1)
                    near = jnp.where(low, el, et) + pltpu.roll(jnp.where(low, ol, ot), 32, 1)
                    far = jnp.where(low, et, eu) + pltpu.roll(jnp.where(low, ot, ou), 32, 1)
                    halves.append(jnp.concatenate([near, far], axis=0))
                d.append(halves)
            for p, (lo_t, hi_t) in enumerate(CLASSES):
                for v in range(2):
                    x = jnp.where(is_t[lo_t], d[hi_t][v], 0.0)
                    if lo_t != hi_t:
                        x = jnp.where(is_t[hi_t], d[lo_t][v], x)
                    rows_s[pl.ds(pl.multiple_of((b * 3 + a) * beads + i0, 16), 16), p * K + v * 128:p * K + (v + 1) * 128] = x.astype(jnp.bfloat16)
    for n in range(1, slots + 1):
        @pl.when(live == n)
        def _(n=n):
            step = groups if n > slots // 2 else 1

            def body(g, carry):
                for q in range(step):
                    for k in range(8):
                        couple((g * step + q) * 16 + k, (g * step + q) * 8 + k, n)
                    if q > 0:
                        unfold(g * step + q - 1)
                unfold(g * step + step - 1)
                return carry
            lax.fori_loop(0, beads // (16 * step), body, 0)

    @pl.when(live == 0)
    def _():
        rows_s[pl.ds(pl.multiple_of(b * 3 * beads, 16), 3 * beads), :] = jnp.zeros((3 * beads, PAIRS * K), jnp.bfloat16)

    @pl.when(b == pl.num_programs(0) - 1)
    def _():
        gram_tiles(me_ref, force_ref, rows_s, left_s, outs, plan)


def design(off, mask, me, strip, below, above, force, plan, groups=4):
    nb, slots = off.shape
    x_rows, by_blocks, _, beads = strip.shape
    total = nb * 3 * beads
    share = (2, plan.pairs, plan.size_x, plan.slots, plan.part, HALF)
    return pl.pallas_call(
        functools.partial(design_kernel, plan=plan, by_blocks=by_blocks, beads=beads, slots=slots, groups=groups),
        grid_spec=pltpu.PrefetchScalarGridSpec(
            num_scalar_prefetch=3,
            grid=(nb,),
            in_specs=[pl.BlockSpec(strip.shape, lambda b, *_: (0, 0, 0, 0))] * 3
            + [pl.BlockSpec((16, total), lambda b, *_: (0, 0))],
            out_specs=[pl.BlockSpec(share, lambda b, *_: (0,) * 6)] * CHUNKS,
            scratch_shapes=[
                pltpu.VMEM((slots, beads, beads), jnp.float32),
                pltpu.VMEM((slots, beads, beads), jnp.float32),
                pltpu.VMEM((slots, beads, beads), jnp.float32),
                pltpu.VMEM((3, slots, beads, beads), jnp.float32),
                pltpu.VMEM((beads // 2 * 72, 128), jnp.float32),
                pltpu.VMEM((total, PAIRS * K), jnp.bfloat16),
                pltpu.VMEM((K, total), jnp.bfloat16),
                pltpu.VMEM((x_rows * (by_blocks + 2), 8, beads), jnp.float32),
                pltpu.VMEM((beads, 8), jnp.float32),
                pltpu.SMEM((slots + 1,), jnp.int32),
            ],
        ),
        out_shape=[jax.ShapeDtypeStruct(share, jnp.float32)] * CHUNKS,
        compiler_params=pltpu.CompilerParams(vmem_limit_bytes=56 * 1024 * 1024),
    )(off, mask, me, strip, below, above, force)


def pack_kernel(me_ref, send_ref, parts_ref, own_ref, *msg_refs, plan, scale):
    def fetch(ref, j, s):
        for z in range(plan.size_x):
            value = parts_ref[s // plan.slots, z ^ me_ref[2], s % plan.slots]
            ref[j, z * plan.part:(z + 1) * plan.part, :] = value * scale

    for s in range(plan.room):
        fetch(own_ref, s, s)
    at = 0
    for ref, count in zip(msg_refs, plan.counts):
        for j in range(count):
            fetch(ref, j, send_ref[me_ref[1], at + j])
        at += count


def pack(me, parts, plan, scale):
    shapes = [(n, HALF // 2, HALF) for n in [plan.room] + plan.counts]
    return pl.pallas_call(
        functools.partial(pack_kernel, plan=plan, scale=scale),
        grid_spec=pltpu.PrefetchScalarGridSpec(
            num_scalar_prefetch=2,
            grid=(1,),
            in_specs=[pl.BlockSpec(parts.shape, lambda b, *_: (0,) * parts.ndim)],
            out_specs=[pl.BlockSpec(s, lambda b, *_: (0, 0, 0)) for s in shapes],
        ),
        out_shape=[jax.ShapeDtypeStruct(s, jnp.float32) for s in shapes],
        compiler_params=pltpu.CompilerParams(vmem_limit_bytes=32 * 1024 * 1024),
    )(me, jnp.asarray(plan.send), parts)


def place_kernel(me_ref, table_ref, rhs_at_ref, mine_ref, other_ref, gram_ref, rhs_ref, full_s, *, plan):
    half = HALF // 2
    core = me_ref[0]
    dev = me_ref[3]
    full_s[:, pl.ds(pl.multiple_of(core * half, half), half), :] = mine_ref[...]
    full_s[:, pl.ds(pl.multiple_of((1 - core) * half, half), half), :] = other_ref[...]
    for u in range(plan.rows // plan.unit):
        at = (dev * plan.rows + u * plan.unit) % HALF
        for c in range(TILES):
            entry = table_ref[dev, u * TILES + c]
            cut = (slice(u * plan.unit, (u + 1) * plan.unit), slice(c * HALF, (c + 1) * HALF))

            @pl.when(entry < 0)
            def _(cut=cut):
                gram_ref[cut] = jnp.zeros((plan.unit, HALF), jnp.float32)

            @pl.when(jnp.logical_and(entry >= 0, entry % 2 == 0))
            def _(cut=cut, entry=entry, at=at):
                gram_ref[cut] = full_s[entry // 2, pl.ds(pl.multiple_of(at, plan.unit), plan.unit), :]

            @pl.when(jnp.logical_and(entry >= 0, entry % 2 == 1))
            def _(cut=cut, entry=entry, at=at):
                turned = full_s[entry // 2].T
                value = turned[0:plan.unit]
                for v in range(1, HALF // plan.unit):
                    value = jnp.where(at == v * plan.unit, turned[v * plan.unit:(v + 1) * plan.unit], value)
                gram_ref[cut] = value
    for u in range(plan.rows // plan.unit):
        at = dev * plan.rows + u * plan.unit
        line = full_s[rhs_at_ref[dev], pl.ds(at // HALF, 1), :]
        value = line[:, 0:plan.unit]
        for v in range(1, HALF // plan.unit):
            value = jnp.where(at % HALF == v * plan.unit, line[:, v * plan.unit:(v + 1) * plan.unit], value)
        rhs_ref[:, u * plan.unit:(u + 1) * plan.unit] = value


def place(me, mine, other, plan):
    return pl.pallas_call(
        functools.partial(place_kernel, plan=plan),
        grid_spec=pltpu.PrefetchScalarGridSpec(
            num_scalar_prefetch=3,
            grid=(1,),
            in_specs=[pl.BlockSpec(mine.shape, lambda b, *_: (0, 0, 0))] * 2,
            out_specs=[
                pl.BlockSpec((plan.rows, PAIRS * K), lambda b, *_: (0, 0)),
                pl.BlockSpec((1, plan.rows), lambda b, *_: (0, 0)),
            ],
            scratch_shapes=[pltpu.VMEM((plan.entries, HALF, HALF), jnp.float32)],
        ),
        out_shape=[
            jax.ShapeDtypeStruct((plan.rows, PAIRS * K), jnp.float32),
            jax.ShapeDtypeStruct((1, plan.rows), jnp.float32),
        ],
        compiler_params=pltpu.CompilerParams(vmem_limit_bytes=32 * 1024 * 1024),
    )(me, jnp.asarray(plan.table), jnp.asarray(plan.rhs), mine, other)


def shifted(x, axis, step):
    count = lax.axis_size(axis)
    return lax.ppermute(x, axis, [(i, (i + step) % count) for i in range(count)])


def swap(x, axis, flip):
    return lax.ppermute(x, axis, [(i, i ^ flip) for i in range(lax.axis_size(axis))])


def summed(x, plan):
    x = x[0] + swap(x[1], "gy", 1)
    got = [swap(x[k], "gy", 2 * k) for k in range(1, plan.pairs)]
    x = functools.reduce(jnp.add, got, x[0])
    got = [swap(x[k], "gx", k) for k in range(1, plan.size_x)]
    x = functools.reduce(jnp.add, got, x[0])
    return jnp.stack([x] + [swap(x, "gx", k) for k in range(1, plan.size_x)])


def shards(coords, kinds, forces, tile_offsets, tile_mask):
    frames, _, blocks_x, blocks_y, beads = coords.shape
    slots = tile_offsets.shape[3]
    nb = blocks_x * blocks_y
    size_x, size_y = lax.axis_size("gx"), lax.axis_size("gy")
    frame_rows = 3 * beads * nb * size_x * size_y
    plan = Plan(size_x, size_y)
    dev = lax.axis_index("gy")
    me = jnp.stack([dev % 2, dev // 2, lax.axis_index("gx"), dev]).astype(jnp.int32)
    cells = jnp.concatenate(
        [jnp.transpose(coords[0], (1, 2, 0, 3)), kinds.astype(jnp.float32)[:, :, None, :]], axis=2
    )
    left, right = shifted(cells, "gx", 1), shifted(cells, "gx", -1)
    strip = jnp.concatenate([left[-1:], cells, right[:1]], axis=0)
    below, above = shifted(strip, "gy", 1), shifted(strip, "gy", -1)
    force = jnp.transpose(forces[0], (1, 2, 0, 3)).reshape(1, nb * 3 * beads)
    chunks = design(
        tile_offsets.reshape(nb, slots),
        tile_mask.reshape(nb, slots),
        me,
        strip,
        below,
        above,
        jnp.broadcast_to(force, (16, nb * 3 * beads)),
        plan,
    )
    parts = jnp.stack([summed(x, plan) for x in chunks])
    own, *messages = pack(me, parts, plan, 1.0 / frame_rows)
    got = [swap(m, "gy", 2 * k) for k, m in enumerate(messages, 1)]
    mine = jnp.concatenate([own] + got)
    gram, rhs = place(me, mine, swap(mine, "gy", 1), plan)
    return gram[None], rhs


def solution(mesh):
    placed = (
        P(None, None, "gx", "gy", None),
        P("gx", "gy", None),
        P(None, None, "gx", "gy", None),
        P(None, "gx", "gy", None),
        P(None, "gx", "gy", None),
    )
    return jax.shard_map(
        shards,
        mesh=mesh,
        in_specs=placed,
        out_specs=(P(None, "gy", None), P(None, "gy")),
        check_vma=False,
    )
```
